128 devices in a mesh: dp: 32 (over x, z, core), tp: 4 (over y).
Axes of the slice: x: 4, y: 4, z: 4, core: 2. Of those that a mesh axis runs over, the one named last changes fastest.
Arguments:
- hidden_in: bfloat16 [8192, 7168], P('dp', 'tp'), may hold values from -6 to 6
- lengths: int32 [32], P('dp'), may hold values from 1 to 256, 4096 in all
- routes: int32 [8192, 8], P('dp'), may hold values from 0 to 255, all different within a row; in each aligned block of 256 rows (0 to 255, 256 to 511, ...) at most 12 rows name the same one
- route_weights: float32 [8192, 8], P('dp'), may hold values from 0.1 to 1
- placement: int32 [32], replicated, may hold values from 0 to 31, each once
- shared_gate: bfloat16 [7168, 1024], P(None, 'tp'), may hold values from -0.0625 to 0.0625
- shared_up: bfloat16 [7168, 1024], P(None, 'tp'), may hold values from -0.0625 to 0.0625
- shared_down: bfloat16 [1024, 7168], P('tp'), may hold values from -0.1875 to 0.1875
- expert_gate: bfloat16 [32, 7168, 1024], P('dp', None, 'tp'), may hold values from -0.0625 to 0.0625
- expert_up: bfloat16 [32, 7168, 1024], P('dp', None, 'tp'), may hold values from -0.0625 to 0.0625
- expert_down: bfloat16 [32, 1024, 7168], P('dp', 'tp'), may hold values from -0.1875 to 0.1875
Outputs:
- moe_out: bfloat16 [8192, 7168], P('dp', 'tp')
The draws below stay inside these ranges and needn't reach their ends.
Inputs may be any that keep to these rules, and one draw needn't show every extreme that they name: `lengths`: one length for each request; they sum to 4096 and the largest is exactly 256. `routes`: each row names 8 different experts; among the 256 rows of one request no expert is named by more than 12 rows, a bound that some block reaches. `placement`: each slot of 0 to 31 holds exactly one expert.
All inputs are finite; a program needn't handle non-finite values. No bound on the sum of `lengths` on one device may be relied on, other than what follows from the above.
Results may differ from the reference program's by a relative error of at most 0.005.
Values may be sent and summed in bfloat16 or wider, within the bound.
A program may use at most 256 MiB of HBM per device.

```python
import math
import jax
import jax.numpy as jnp
import numpy as np
from jax import lax

D = 7168
SH_FF = 1024
MOE_FF = 1024
ROUTED = 256
TOPK = 8
TOK_AVG = 128
CAP = 256
MOST_R = 12
EXPERTS = 32
ROWS = 8192
N_DP = 32


def block_scale(stream_key, dims, pieces, least, top_value):
    def one(axis_at, blocks):
        heights = jax.random.uniform(jax.random.fold_in(jax.random.fold_in(stream_key, 6), axis_at), (blocks,), jnp.float32, least / len(pieces), top_value / len(pieces))
        return jnp.repeat(jnp.exp(heights), dims[axis_at] // blocks).reshape((-1,) + (1,) * (len(dims) - axis_at - 1))

    loudness = one(*pieces[0])
    for cut in pieces[1:]:
        loudness = loudness * one(*cut)
    return loudness


def profile(number_of, total, limit, slope):
    weights = [(1 << 20) // math.isqrt(standing ** slope) + 1 for standing in range(2, number_of + 1)]
    surplus, holding = total - limit - (number_of - 1), [1] * (number_of - 1)
    while surplus > 0:
        candidates = [i for i in range(number_of - 1) if holding[i] < limit]
        pool, left = sum([weights[i] for i in candidates]), surplus
        for i in candidates:
            more = min(limit - holding[i], max(1, left * weights[i] // pool), surplus)
            holding[i] = holding[i] + more
            surplus = surplus - more
    return np.array([limit] + holding)


def ragged_sizes(stream_key, number_of, total, bound, skew):
    if number_of == 2:
        one = jax.random.randint(stream_key, (), max(1, total - bound), min(bound, total - 1) + 1)
        return jnp.stack([one, total - one])
    sizes = jnp.asarray(profile(number_of, total, bound, skew), jnp.int32)
    couples = (number_of - 1) // 2
    giver, sink = sizes[1:1 + 2 * couples:2], sizes[2:2 + 2 * couples:2]
    slack = jnp.minimum(giver - 1, bound - sink)
    moved = jax.random.randint(jax.random.fold_in(stream_key, 1), (couples,), 0, 1 << 20) % (slack + 1)
    sizes = sizes.at[1:1 + 2 * couples:2].set(giver - moved).at[2:2 + 2 * couples:2].set(sink + moved)
    return sizes[jax.random.permutation(jax.random.fold_in(stream_key, 2), number_of)]


def assign_block(key, own, number, rows, amount, top, most, skew):
    sequence = jax.random.permutation(key, amount)
    heavy_load, ordinary = shares(amount, rows * top, most, skew, True), shares(amount, rows * top, most, skew, False)
    places = jnp.arange(amount)

    def named(sizes, rotation):
        used = int((sizes > 0).sum())
        fixed = max(1, used // 4)
        passed = fixed + (places - fixed + rotation * (used - fixed)) % max(1, amount - fixed)
        return jnp.zeros((amount,), jnp.int32).at[sequence[jnp.where(places < fixed, places, passed)]].set(jnp.asarray(sizes, jnp.int32))

    sizes = jnp.where(number % 4 == 0, named(heavy_load, number // 4), named(ordinary, number - number // 4 - 1))
    mixed = jax.random.permutation(jax.random.fold_in(own, 3), amount)
    source_of, receiver = mixed[0:amount // 2 * 2:2], mixed[1:amount // 2 * 2:2]
    slack = jnp.minimum(sizes[source_of] - 1, most - sizes[receiver]) // 2
    slack = jnp.where((source_of == sequence[0]) | (receiver == sequence[0]) | (sizes[receiver] == 0), 0, jnp.maximum(slack, 0))
    passed = jax.random.randint(jax.random.fold_in(own, 4), (amount // 2,), 0, 1 << 20) % (slack + 1)
    sizes = sizes.at[source_of].add(-passed).at[receiver].add(passed)
    items = jnp.searchsorted(jnp.cumsum(sizes), jnp.arange(rows * top), side="right").astype(jnp.int32)
    listing = items.reshape(top, rows).T
    listing = listing[jax.random.permutation(jax.random.fold_in(own, 1), rows)]
    rotation = jax.random.randint(jax.random.fold_in(own, 2), (rows, 1), 0, top)
    return jnp.take_along_axis(listing, (jnp.arange(top)[None, :] + rotation) % top, axis=1)


def shares(amount, total, limit, lean, full):
    weights = [(1 << 20) // math.isqrt(rank ** lean) + 1 for rank in range(1, amount + 1)]
    largest = limit if full else min(limit, max(-(-total // amount), total * weights[0] // sum(weights)))
    least = 1 if total - largest >= amount - 1 else 0
    given, surplus = [largest] + [least] * (amount - 1), total - largest - least * (amount - 1)
    while surplus > 0:
        free = [i for i in range(1, amount) if given[i] < largest] or [i for i in range(1, amount) if given[i] < limit]
        mass, remaining = sum([weights[i] for i in free]), surplus
        for i in free:
            addition = min(limit - given[i], max(1, remaining * weights[i] // mass), surplus)
            given[i] = given[i] + addition
            surplus = surplus - addition
    return np.array(given)


def scatter_about(stream_key, extent, spread, most, cuts=(), kind=jnp.bfloat16):
    factor_of = block_scale(stream_key, extent, cuts, -0.22, 0.18) if cuts else 1.0
    values = jax.random.normal(stream_key, extent, jnp.float32) * spread * factor_of
    return jnp.minimum(jnp.maximum(values, -most), most).astype(kind)


def setup_inputs(seed: int = 0) -> dict:
    key_list = jax.random.split(jax.random.key(seed), 12)
    hidden_in = scatter_about(key_list[0], (ROWS, D), 1.0, 6.0, ((0, 32), (1, 4)))
    lengths = ragged_sizes(key_list[1], N_DP, TOK_AVG * N_DP, CAP, 2).astype(jnp.int32)
    routes_keys = jax.random.split(jax.random.fold_in(key_list[2], 1), ROWS // CAP)
    routes_turns = jax.random.permutation(jax.random.fold_in(key_list[2], 3), ROWS // CAP)
    routes = jax.vmap(lambda own, number: assign_block(jax.random.fold_in(key_list[2], 2), own, number, CAP, ROUTED, TOPK, MOST_R, 2))(routes_keys, routes_turns).reshape((ROWS, TOPK))
    route_weights = jnp.clip(jnp.exp(math.log(1.0) - 2.3025851 * jax.random.uniform(key_list[3], (ROWS, TOPK), jnp.float32) ** block_scale(key_list[3], (ROWS, TOPK), ((0, 32),), -0.2, 0.2)), 0.1, 1.0)
    placement = jax.random.permutation(key_list[4], EXPERTS).astype(jnp.int32)
    shared_gate = scatter_about(key_list[5], (D, SH_FF), D ** -0.5, 0.0625, ((1, 4),))
    shared_up = scatter_about(key_list[6], (D, SH_FF), D ** -0.5, 0.0625, ((1, 4),))
    shared_down = scatter_about(key_list[7], (SH_FF, D), SH_FF ** -0.5, 0.1875, ((0, 4),))
    expert_gate = scatter_about(key_list[8], (EXPERTS, D, MOE_FF), D ** -0.5, 0.0625, ((0, 32), (2, 4)))
    expert_up = scatter_about(key_list[9], (EXPERTS, D, MOE_FF), D ** -0.5, 0.0625, ((0, 32), (2, 4)))
    expert_down = scatter_about(key_list[10], (EXPERTS, MOE_FF, D), MOE_FF ** -0.5, 0.1875, ((0, 32), (1, 4)))
    return dict(hidden_in=hidden_in, lengths=lengths, routes=routes, route_weights=route_weights, placement=placement, shared_gate=shared_gate, shared_up=shared_up, shared_down=shared_down, expert_gate=expert_gate, expert_up=expert_up, expert_down=expert_down)


def swiglu(inputs, gate_matrix, up_matrix):
    gate_part = jnp.dot(inputs, gate_matrix, preferred_element_type=jnp.float32)
    up_part = jnp.dot(inputs, up_matrix, preferred_element_type=jnp.float32)
    return (jax.nn.silu(gate_part) * up_part).astype(jnp.bfloat16)


def reference(hidden_in, lengths, routes, route_weights, placement, shared_gate, shared_up, shared_down, expert_gate, expert_up, expert_down):
    row_count = hidden_in.shape[0]
    row_index = jnp.arange(row_count, dtype=jnp.int32)
    request = row_index // CAP
    is_live = (row_index % CAP) < lengths[request]
    shared_hidden = swiglu(hidden_in, shared_gate, shared_up)
    shared = jnp.dot(shared_hidden, shared_down, preferred_element_type=jnp.float32)
    capacity = N_DP * MOST_R

    def one_expert(routed, expert):
        matches = (routes == expert) & is_live[:, None]
        is_named = jnp.any(matches, axis=1)
        scales = jnp.sum(jnp.where(matches, route_weights, jnp.zeros_like(route_weights)), axis=1)
        chosen = jnp.nonzero(is_named, size=capacity, fill_value=0)[0].astype(jnp.int32)
        filled = jnp.arange(capacity, dtype=jnp.int32) < jnp.sum(is_named.astype(jnp.int32))
        holder = placement[expert]
        inner_rows = swiglu(hidden_in[chosen], expert_gate[holder], expert_up[holder])
        result = jnp.dot(inner_rows, expert_down[holder], preferred_element_type=jnp.float32)
        picked_scales = scales[chosen]
        factor = jnp.where(filled, picked_scales, jnp.zeros_like(picked_scales))
        return routed.at[chosen].add(result * factor[:, None]), None

    routed, unused = lax.scan(one_expert, jnp.zeros(shared.shape, jnp.float32), jnp.arange(EXPERTS, dtype=jnp.int32))
    combined = shared + routed
    return jnp.where(is_live[:, None], combined, jnp.zeros_like(combined)).astype(jnp.bfloat16)
```

```python
import jax
import jax.numpy as jnp
from jax import lax
from jax.sharding import PartitionSpec as P

MOST_R = 12


def gated_hidden(gate_total, up_total):
    return (jax.nn.silu(gate_total) * up_total).astype(jnp.bfloat16)


def local(
    hidden_in,
    lengths,
    routes,
    route_weights,
    placement,
    shared_gate,
    shared_up,
    shared_down,
    expert_gate,
    expert_up,
    expert_down,
):
    rank_rows = hidden_in.shape[0]
    quarter = hidden_in.shape[1]
    groups = lax.axis_size("dp")
    slices = lax.axis_size("tp")
    full_width = quarter * slices
    window = placement.shape[0]
    per_peer = MOST_R
    slot_count = groups * per_peer
    is_live = jnp.arange(rank_rows, dtype=jnp.int32) < lengths[0]
    shard_cols = lax.all_gather(hidden_in, "tp", axis=1, tiled=True)
    gate_rows = shared_gate
    up_rows = shared_up
    shared_gate_sum = jnp.dot(shard_cols, gate_rows, preferred_element_type=jnp.float32)
    shared_up_sum = jnp.dot(shard_cols, up_rows, preferred_element_type=jnp.float32)
    shared_part = jnp.dot(
        gated_hidden(shared_gate_sum, shared_up_sum),
        shared_down,
        preferred_element_type=jnp.float32,
    )
    in_window = (routes < window) & is_live[:, None]
    expert_ids = jnp.where(in_window, routes, 0)
    matches = (
        expert_ids[:, :, None] == jnp.arange(window, dtype=jnp.int32)[None, None, :]
    ) & in_window[:, :, None]
    hit_counts = matches.astype(jnp.int32)
    per_row = jnp.sum(hit_counts, axis=1)
    earlier = jnp.cumsum(per_row, axis=0) - per_row
    position = jnp.sum(hit_counts * earlier[:, None, :], axis=2)
    holder = jnp.sum(hit_counts * placement[None, None, :], axis=2)
    target = jnp.where(in_window, holder * per_peer + position, -1)
    picked = target[:, :, None] == jnp.arange(slot_count, dtype=jnp.int32)[None, None, :]
    selector = jnp.any(picked, axis=1).astype(jnp.bfloat16)
    outgoing = jnp.einsum(
        "cs,cq->sq", selector, hidden_in, preferred_element_type=jnp.float32
    ).astype(jnp.bfloat16)
    arrived = lax.all_to_all(
        outgoing.reshape(groups, per_peer, quarter), "dp", split_axis=0, concat_axis=0, tiled=True
    )
    shard_cols = lax.all_gather(arrived.reshape(slot_count, quarter), "tp", axis=1, tiled=True)
    gate_rows = expert_gate[0]
    up_rows = expert_up[0]
    expert_gate_sum = jnp.dot(shard_cols, gate_rows, preferred_element_type=jnp.float32)
    expert_up_sum = jnp.dot(shard_cols, up_rows, preferred_element_type=jnp.float32)
    expert_part = jnp.dot(
        gated_hidden(expert_gate_sum, expert_up_sum),
        expert_down[0],
        preferred_element_type=jnp.float32,
    )
    rows_back = lax.all_to_all(
        expert_part.astype(jnp.bfloat16), "tp", split_axis=1, concat_axis=0, tiled=True
    ).reshape(slices, slot_count, quarter)
    expert_sum = jnp.sum(rows_back.astype(jnp.float32), axis=0).astype(jnp.bfloat16)
    came_back = lax.all_to_all(
        expert_sum.reshape(groups, per_peer, quarter),
        "dp",
        split_axis=0,
        concat_axis=0,
        tiled=True,
    ).reshape(slot_count, quarter)
    shared_rows = lax.all_to_all(
        shared_part.astype(jnp.bfloat16), "tp", split_axis=1, concat_axis=0, tiled=True
    ).reshape(slices, rank_rows, quarter)
    shared_sum = jnp.sum(shared_rows.astype(jnp.float32), axis=0)
    weight_of = jnp.sum(jnp.where(picked, route_weights[:, :, None], 0.0), axis=1)
    coarse = weight_of.astype(jnp.bfloat16)
    fine = (weight_of - coarse.astype(jnp.float32)).astype(jnp.bfloat16)
    combined = (
        shared_sum
        + jnp.dot(coarse, came_back, preferred_element_type=jnp.float32)
        + jnp.dot(fine, came_back, preferred_element_type=jnp.float32)
    )
    return jnp.where(is_live[:, None], combined, 0.0).astype(jnp.bfloat16)


def solution(mesh):
    in_specs = (
        P("dp", "tp"),
        P("dp"),
        P("dp", None),
        P("dp", None),
        P(),
        P(None, "tp"),
        P(None, "tp"),
        P("tp", None),
        P("dp", None, "tp"),
        P("dp", None, "tp"),
        P("dp", "tp", None),
    )
    out_specs = P("dp", "tp")
    return jax.shard_map(local, mesh=mesh, in_specs=in_specs, out_specs=out_specs, check_vma=False)
```

```python
import functools

import jax
import jax.numpy as jnp
from jax import lax
from jax.experimental import pallas as pl
from jax.experimental.pallas import tpu as pltpu
from jax.sharding import PartitionSpec as P

MOST_R = 12
MESH = pl.DeviceIdType.MESH
BF16 = jnp.bfloat16
F32 = jnp.float32
TP = 4
CHUNKS = 4


def dot(a, b):
    return jnp.dot(a, b, preferred_element_type=F32)


def silu(v):
    return v / (1.0 + jnp.exp(-v))


def slot_parts(shape, axis):
    at = lax.broadcasted_iota(jnp.int32, shape, axis)
    group = (at * 2731) >> 16
    place = at - group * (2 * MOST_R)
    half = (place >= MOST_R).astype(jnp.int32)
    return group, half, place - MOST_R * half


def kernel(
    groups,
    routes_ref,
    routes_t_ref,
    weights_ref,
    placement_row_ref,
    placement_col_ref,
    length_ref,
    hidden_ref,
    sg_ref,
    su_ref,
    sd_ref,
    eg_ref,
    eu_ref,
    ed_ref,
    out_ref,
    wsgu,
    wsd,
    wgu,
    wed,
    held,
    sel,
    back_hi,
    back_lo,
    outgoing,
    arrived,
    acc,
    shared_acc,
    hid2,
    s_part,
    s_own,
    s_relay,
    s_left,
    s_right,
    e_relay,
    e_left,
    e_right,
    came,
    w_sem,
    ag_send,
    ag_recv,
    d_send,
    d_recv,
    d_loc,
    s_send,
    s_recv,
    e_send,
    e_recv,
    c_sem,
):
    dp = lax.axis_index("dp")
    tp = lax.axis_index("tp")
    right = lax.rem(tp + 1, TP)
    left = lax.rem(tp + TP - 1, TP)
    across = lax.rem(tp + 2, TP)
    rows = held.shape[1] // 2
    wide = held.shape[2]
    window = placement_row_ref.shape[1]
    hidden_units = ed_ref.shape[0]
    per_chunk = groups // CHUNKS
    chunk_rows = per_chunk * 2 * MOST_R
    packed = groups * 2 * MOST_R
    top = routes_ref.shape[1]
    owners = (tp, left, right, across)

    for half in range(2):
        pltpu.make_async_copy(
            hidden_ref.at[:, pl.ds(half * wide, wide)],
            held.at[0, pl.ds(half * rows, rows)],
            w_sem.at[0],
        ).start()
    for at, (gate, up, both) in enumerate(((sg_ref, su_ref, wsgu), (eg_ref, eu_ref, wgu))):
        for part, source in enumerate((gate, up)):
            pltpu.make_async_copy(
                source,
                both.at[:, :, pl.ds(part * hidden_units, hidden_units)],
                w_sem.at[1 + at],
            ).start()
    for at, (down, kept) in enumerate(((sd_ref, wsd), (ed_ref, wed))):
        for piece in range(2 * TP):
            pltpu.make_async_copy(
                down.at[:, pl.ds(piece * wide, wide)],
                kept.at[piece // 2, pl.ds((piece % 2) * hidden_units, hidden_units)],
                w_sem.at[3 + at],
            ).start()

    def arrived_weights(ref, at):
        pltpu.make_async_copy(ref, ref, w_sem.at[at]).wait()

    barrier = pltpu.get_barrier_semaphore()

    @pl.loop(1, groups)
    def _(step):
        pl.semaphore_signal(
            barrier,
            inc=1,
            device_id=(lax.rem(dp + step, groups), tp),
            device_id_type=MESH,
        )

    for neighbour in (left, right):
        pl.semaphore_signal(barrier, inc=1, device_id=(dp, neighbour), device_id_type=MESH)

    length = length_ref[0]
    live = lax.broadcasted_iota(jnp.int32, (window, rows), 1) < length
    expert_at = lax.broadcasted_iota(jnp.int32, (window, rows), 0)
    named = jnp.zeros((window, rows), F32)
    for k in range(top):
        named = named + jnp.where(routes_t_ref[pl.ds(k, 1), :] == expert_at, 1.0, 0.0)
    named = jnp.where(live, named, 0.0)
    before = jnp.where(
        lax.broadcasted_iota(jnp.int32, (rows, rows), 0)
        < lax.broadcasted_iota(jnp.int32, (rows, rows), 1),
        1.0,
        0.0,
    ).astype(BF16)
    place = jnp.where(named > 0.0, dot(named.astype(BF16), before), -1.0).astype(BF16)
    group_of, _, _ = slot_parts((packed, window), 0)
    spread = jnp.where(placement_row_ref[...] == group_of, 1.0, 0.0).astype(BF16)
    _, half_of, want = slot_parts((packed, rows), 0)
    hit = dot(spread, place) == want.astype(F32)
    for half in range(2):
        sel[:, pl.ds(half * rows, rows)] = jnp.where(
            hit, jnp.where(half_of == half, 1.0, 0.0), 0.0
        ).astype(BF16)

    pl.semaphore_wait(barrier, groups - 1 + 2)

    def to(src, dst, send, recv, device):
        return pltpu.make_async_remote_copy(
            src_ref=src,
            dst_ref=dst,
            send_sem=send,
            recv_sem=recv,
            device_id=device,
            device_id_type=MESH,
        )

    arrived_weights(held.at[0], 0)

    def half_block(slot, half):
        return held.at[slot, pl.ds(half * rows, rows)]

    gathers = []
    for at, (source, target, half, device) in enumerate(
        (
            (0, 1, 0, right),
            (0, 2, 1, left),
            (0, 1, 1, right),
            (0, 2, 0, left),
            (1, 3, 0, right),
            (2, 3, 1, left),
        )
    ):
        gathers.append(
            to(
                half_block(source, half),
                half_block(target, half),
                ag_send.at[at],
                ag_recv.at[at],
                (dp, device),
            )
        )
    for at in range(4):
        gathers[at].start()

    my_chunk = dp // per_chunk

    def chunk_at(k):
        return lax.rem(my_chunk + k, CHUNKS)

    def send_chunk(source, landing, chunk, send, recv, local):
        @pl.loop(0, per_chunk)
        def _(step):
            target = chunk * per_chunk + lax.rem(dp + step, per_chunk)

            @pl.when(target != dp)
            def _():
                to(source.at[target], landing.at[dp], send, recv, (target, tp)).start()

            @pl.when(target == dp)
            def _():
                pltpu.make_async_copy(source.at[dp], landing.at[dp], local).start()

    def wait_peers(ref, sem):
        view = ref.at[pl.ds(0, groups - 1)]
        pltpu.make_async_copy(view, view, sem).wait()

    def select(slot):
        @pl.loop(0, CHUNKS)
        def _(k):
            chunk = chunk_at(k)
            picked = dot(
                sel[pl.ds(pl.multiple_of(chunk * chunk_rows, chunk_rows), chunk_rows), :],
                held[slot],
            )
            outgoing[slot, pl.ds(chunk * per_chunk, per_chunk)] = picked.reshape(
                per_chunk, 2 * MOST_R, wide
            ).astype(BF16)
            send_chunk(
                outgoing.at[slot],
                arrived.at[slot],
                chunk,
                d_send.at[slot],
                d_recv.at[slot],
                d_loc.at[slot],
            )

    def shared_step(slot):
        owner = owners[slot]
        total = dot(held[slot, pl.ds(0, rows)], wsgu[2 * owner]) + dot(
            held[slot, pl.ds(rows, rows)], wsgu[2 * owner + 1]
        )
        if slot == 0:
            shared_acc[...] = total
        else:
            shared_acc[...] += total

    def load_chunk(ref, k):
        return ref[pl.ds(k * per_chunk, per_chunk)].astype(F32).reshape(chunk_rows, wide)

    def rows_of(chunk):
        return pl.ds(pl.multiple_of(chunk * chunk_rows, chunk_rows), chunk_rows)

    select(0)
    arrived_weights(wsgu, 1)
    shared_step(0)

    expert_at = lax.broadcasted_iota(jnp.int32, (rows, window), 1)
    live = lax.broadcasted_iota(jnp.int32, (rows, window), 0) < length
    named = jnp.zeros((rows, window), F32)
    scale = jnp.zeros((rows, window), F32)
    for k in range(top):
        match = routes_ref[:, pl.ds(k, 1)] == expert_at
        named = named + jnp.where(match, 1.0, 0.0)
        scale = scale + jnp.where(match, weights_ref[:, pl.ds(k, 1)], 0.0)
    named = jnp.where(live, named, 0.0)
    before = jnp.where(
        lax.broadcasted_iota(jnp.int32, (rows, rows), 1)
        < lax.broadcasted_iota(jnp.int32, (rows, rows), 0),
        1.0,
        0.0,
    ).astype(BF16)
    place = jnp.where(named > 0.0, dot(before, named.astype(BF16)), -1.0).astype(BF16)
    group_of, _, _ = slot_parts((window, packed), 1)
    spread = jnp.where(placement_col_ref[...] == group_of, 1.0, 0.0).astype(BF16)
    _, half_of, want = slot_parts((rows, packed), 1)
    hit = dot(place, spread) == want.astype(F32)
    head = scale.astype(BF16)
    rest = (scale - head.astype(F32)).astype(BF16)
    for part, kept in ((head, back_hi), (rest, back_lo)):
        value = jnp.where(hit, dot(part, spread), 0.0)
        for half in range(2):
            kept[pl.ds(half * rows, rows), :] = jnp.where(half_of == half, value, 0.0).astype(BF16)

    for at in (0, 1):
        gathers[at].wait_recv()
        gathers[at + 4].start()
    for slot in (1, 2):
        gathers[slot + 1].wait_recv()
        select(slot)
        shared_step(slot)
    for at in (4, 5):
        gathers[at].wait_recv()
    select(3)
    shared_step(3)

    shared_hidden = (
        silu(shared_acc[:, pl.ds(0, hidden_units)])
        * shared_acc[:, pl.ds(hidden_units, hidden_units)]
    ).astype(BF16)
    arrived_weights(wsd, 3)
    for at, owner in ((0, across), (1, right), (2, left), (3, tp)):
        for half in range(2):
            part = dot(shared_hidden, wsd[owner, pl.ds(half * hidden_units, hidden_units)])
            if at < 3:
                s_part[at, pl.ds(half * rows, rows)] = part.astype(BF16)
            else:
                s_own[pl.ds(half * rows, rows)] = part

    def s_copy(at, part, half, landing, device):
        where = pl.ds(half * rows, rows)
        return to(
            s_part.at[part, where],
            landing.at[where],
            s_send.at[at],
            s_recv.at[at],
            (dp, device),
        )

    shared_sends = [
        s_copy(0, 0, 0, s_relay, right),
        s_copy(1, 0, 1, s_relay, left),
        s_copy(2, 1, 1, s_left, right),
        s_copy(3, 2, 0, s_right, left),
        s_copy(4, 1, 0, s_left, right),
        s_copy(5, 2, 1, s_right, left),
    ]
    for at in range(4):
        shared_sends[at].start()

    both = 2 * hidden_units

    def expert_step(slot):
        wait_peers(arrived.at[slot], d_recv.at[slot])
        pltpu.make_async_copy(arrived.at[slot, 0], arrived.at[slot, 0], d_loc.at[slot]).wait()
        owner = owners[slot]

        @pl.loop(0, CHUNKS)
        def _(k):
            block = load_chunk(arrived.at[slot], k).astype(BF16)
            for half in range(2):
                where = (rows_of(k), pl.ds(half * both, both))
                total = dot(block, wgu[2 * owner + half])
                if slot == 0:
                    acc[where] = total
                else:
                    acc[where] += total

    arrived_weights(wgu, 2)
    expert_step(0)
    for at, part, half in ((0, 1, 0), (1, 2, 1)):
        shared_sends[at].wait_recv()
        where = pl.ds(half * rows, rows)
        s_part[part, where] = (
            s_part[part, where].astype(F32) + s_relay[where].astype(F32)
        ).astype(BF16)
        shared_sends[at + 4].start()
    expert_step(1)
    expert_step(2)
    arrived_weights(wed, 4)
    for at in range(2, 6):
        shared_sends[at].wait_recv()
    s_own[...] = s_own[...] + s_left[...].astype(F32) + s_right[...].astype(F32)
    for slot in range(4):
        wait_peers(outgoing.at[slot], d_send.at[slot])
    expert_step(3)

    @pl.loop(0, CHUNKS)
    def _(k):
        first = acc[rows_of(k), pl.ds(0, both)]
        second = acc[rows_of(k), pl.ds(both, both)]
        total = first + pltpu.roll(second, chunk_rows - MOST_R, 0)
        inner = silu(total[:, :hidden_units]) * total[:, hidden_units:]
        _, half_of, _ = slot_parts((chunk_rows, hidden_units), 0)
        hid2[rows_of(k), pl.ds(0, hidden_units)] = jnp.where(half_of == 0, inner, 0.0).astype(BF16)
        hid2[rows_of(k), pl.ds(hidden_units, hidden_units)] = jnp.where(
            half_of == 1, pltpu.roll(inner, MOST_R, 0), 0.0
        ).astype(BF16)

    def down(slot, owner, k):
        chunk = chunk_at(k)
        part = dot(hid2[rows_of(chunk), :], wed[owner])
        if slot:
            outgoing[slot, pl.ds(chunk * per_chunk, per_chunk)] = part.reshape(
                per_chunk, 2 * MOST_R, wide
            ).astype(BF16)
        else:
            acc[rows_of(chunk), pl.ds(0, wide)] = part

    def e_copy(at, slot, k, landing, device):
        where = pl.ds(chunk_at(k) * per_chunk, per_chunk)
        return to(
            outgoing.at[slot, where],
            landing.at[where],
            e_send.at[at],
            e_recv.at[at],
            (dp, device),
        )

    relays = [e_copy(k, 1, k, e_relay, right if k < 2 else left) for k in range(4)]
    directs = [
        e_copy(4 + k, 3 if k < 2 else 2, k, e_right if k < 2 else e_left, left if k < 2 else right)
        for k in range(4)
    ]
    passed = [
        e_copy(8 + k, 2 if k < 2 else 3, k, e_left if k < 2 else e_right, right if k < 2 else left)
        for k in range(4)
    ]
    for k in (0, 2, 1, 3):
        down(1, across, k)
        relays[k].start()
    for k in (2, 0, 3, 1):
        down(2 if k >= 2 else 3, right if k >= 2 else left, k)
        directs[k].start()
    for k in (0, 2, 1, 3):
        down(2 if k < 2 else 3, right if k < 2 else left, k)
    for k in (0, 2, 1, 3):
        slot = 2 if k < 2 else 3
        where = pl.ds(chunk_at(k) * per_chunk, per_chunk)
        relays[k].wait_recv()
        outgoing[slot, where] = (
            outgoing[slot, where].astype(F32) + e_relay[where].astype(F32)
        ).astype(BF16)
        passed[k].start()
    for k in (0, 2, 1, 3):
        down(0, tp, k)
    for k in (0, 2, 1, 3):
        chunk = chunk_at(k)
        directs[k].wait_recv()
        passed[k].wait_recv()
        total = (
            acc[rows_of(chunk), pl.ds(0, wide)]
            + load_chunk(e_left, chunk)
            + load_chunk(e_right, chunk)
        )
        outgoing[0, pl.ds(chunk * per_chunk, per_chunk)] = total.reshape(
            per_chunk, 2 * MOST_R, wide
        ).astype(BF16)
        send_chunk(outgoing.at[0], came, chunk, c_sem.at[0], c_sem.at[1], c_sem.at[2])

    wait_peers(came, c_sem.at[1])
    pltpu.make_async_copy(came.at[0], came.at[0], c_sem.at[2]).wait()
    for k in range(CHUNKS):
        block = load_chunk(came, k).astype(BF16)
        where = pl.ds(k * chunk_rows, chunk_rows)
        s_own[...] += dot(back_hi[:, where], block) + dot(back_lo[:, where], block)
    keep = lax.broadcasted_iota(jnp.int32, (rows, wide), 0) < length
    for half in range(2):
        out_ref[:, pl.ds(half * wide, wide)] = jnp.where(
            keep, s_own[pl.ds(half * rows, rows)], 0.0
        ).astype(out_ref.dtype)

    for copy in gathers + shared_sends + relays + directs + passed:
        copy.wait_send()
    wait_peers(outgoing.at[0], c_sem.at[0])


def local(
    hidden_in,
    lengths,
    routes,
    route_weights,
    placement,
    shared_gate,
    shared_up,
    shared_down,
    expert_gate,
    expert_up,
    expert_down,
):
    groups = lax.axis_size("dp")
    rows, quarter = hidden_in.shape
    wide = quarter // 2
    pieces = 2 * TP
    units = shared_gate.shape[1]
    window = placement.shape[0]
    packed = groups * 2 * MOST_R
    across_peers = (groups, 2 * MOST_R, wide)
    vmem = pl.BlockSpec(memory_space=pltpu.VMEM)
    smem = pl.BlockSpec(memory_space=pltpu.SMEM)
    hbm = pl.BlockSpec(memory_space=pl.ANY)
    dma = pltpu.SemaphoreType.DMA
    return pl.pallas_call(
        functools.partial(kernel, groups),
        out_shape=jax.ShapeDtypeStruct((rows, quarter), BF16),
        in_specs=[vmem] * 5 + [smem] + [hbm] * 7,
        out_specs=vmem,
        scratch_shapes=[
            pltpu.VMEM((pieces, wide, 2 * units), BF16),
            pltpu.VMEM((TP, 2 * units, wide), BF16),
            pltpu.VMEM((pieces, wide, 2 * units), BF16),
            pltpu.VMEM((TP, 2 * units, wide), BF16),
            pltpu.VMEM((TP, 2 * rows, wide), BF16),
            pltpu.VMEM((packed, 2 * rows), BF16),
            pltpu.VMEM((2 * rows, packed), BF16),
            pltpu.VMEM((2 * rows, packed), BF16),
            pltpu.VMEM((TP,) + across_peers, BF16),
            pltpu.VMEM((TP,) + across_peers, BF16),
            pltpu.VMEM((packed, 4 * units), F32),
            pltpu.VMEM((rows, 2 * units), F32),
            pltpu.VMEM((packed, 2 * units), BF16),
            pltpu.VMEM((3, 2 * rows, wide), BF16),
            pltpu.VMEM((2 * rows, wide), F32),
            pltpu.VMEM((2 * rows, wide), BF16),
            pltpu.VMEM((2 * rows, wide), BF16),
            pltpu.VMEM((2 * rows, wide), BF16),
            pltpu.VMEM(across_peers, BF16),
            pltpu.VMEM(across_peers, BF16),
            pltpu.VMEM(across_peers, BF16),
            pltpu.VMEM(across_peers, BF16),
            dma((5,)),
            dma((6,)),
            dma((6,)),
            dma((TP,)),
            dma((TP,)),
            dma((TP,)),
            dma((6,)),
            dma((6,)),
            dma((12,)),
            dma((12,)),
            dma((3,)),
        ],
        compiler_params=pltpu.CompilerParams(
            collective_id=0, has_side_effects=True, vmem_limit_bytes=62 << 20
        ),
        cost_estimate=pl.CostEstimate(
            flops=2 * 5 * rows * quarter * 4 * units * 3 // 2,
            bytes_accessed=6 * quarter * 4 * units * 2,
            transcendentals=0,
        ),
    )(
        routes,
        routes.T,
        route_weights,
        placement.reshape(1, window),
        placement.reshape(window, 1),
        lengths,
        hidden_in,
        shared_gate.reshape(pieces, wide, units),
        shared_up.reshape(pieces, wide, units),
        shared_down,
        expert_gate.reshape(pieces, wide, units),
        expert_up.reshape(pieces, wide, units),
        expert_down[0],
    )


def solution(mesh):
    in_specs = (
        P("dp", "tp"),
        P("dp"),
        P("dp", None),
        P("dp", None),
        P(),
        P(None, "tp"),
        P(None, "tp"),
        P("tp", None),
        P("dp", None, "tp"),
        P("dp", None, "tp"),
        P("dp", "tp", None),
    )
    out_specs = P("dp", "tp")
    return jax.shard_map(local, mesh=mesh, in_specs=in_specs, out_specs=out_specs, check_vma=False)
```

```python
import functools

import jax
import jax.numpy as jnp
from jax import lax
from jax.experimental import pallas as pl
from jax.experimental.pallas import tpu as pltpu
from jax.sharding import PartitionSpec as P

MOST_R = 12
MESH = pl.DeviceIdType.MESH
BF16 = jnp.bfloat16
F32 = jnp.float32
TP = 4
CHUNKS = 4


def dot(a, b):
    return jnp.dot(a, b, preferred_element_type=F32)


def silu(v):
    return v / (1.0 + jnp.exp(-v))


def slot_parts(shape, axis):
    at = lax.broadcasted_iota(jnp.int32, shape, axis)
    group = (at * 2731) >> 16
    place = at - group * (2 * MOST_R)
    half = (place >= MOST_R).astype(jnp.int32)
    return group, half, place - MOST_R * half


def kernel(
    groups,
    routes_ref,
    weights_ref,
    placement_ref,
    length_ref,
    hidden_ref,
    sg_ref,
    su_ref,
    sd_ref,
    eg_ref,
    eu_ref,
    ed_ref,
    out_ref,
    wsgu,
    wsd,
    wgu,
    wed,
    held,
    sel,
    back_hi,
    back_lo,
    outgoing,
    arrived,
    acc,
    shared_acc,
    hid2,
    s_part,
    s_own,
    s_relay,
    s_left,
    s_right,
    e_relay,
    e_left,
    e_right,
    came,
    w_sem,
    ag_send,
    ag_recv,
    d_send,
    d_recv,
    d_loc,
    s_send,
    s_recv,
    e_send,
    e_recv,
    c_send,
    c_recv,
    c_loc,
):
    dp = lax.axis_index("dp")
    tp = lax.axis_index("tp")
    right = lax.rem(tp + 1, TP)
    left = lax.rem(tp + TP - 1, TP)
    across = lax.rem(tp + 2, TP)
    rows = held.shape[1] // 2
    wide = held.shape[2]
    window = placement_ref.shape[1]
    hidden_units = ed_ref.shape[0]
    per_chunk = groups // CHUNKS
    chunk_rows = per_chunk * 2 * MOST_R
    packed = groups * 2 * MOST_R
    top = routes_ref.shape[0]
    pieces = (
        (2 * tp, 2 * tp + 1),
        (2 * left, 2 * right + 1),
        (2 * left + 1, 2 * right),
        (2 * across, 2 * across + 1),
    )

    for half in range(2):
        pltpu.make_async_copy(
            hidden_ref.at[:, pl.ds(half * wide, wide)],
            held.at[0, pl.ds(half * rows, rows)],
            w_sem.at[0],
        ).start()
    for at, (gate, up, both) in enumerate(((sg_ref, su_ref, wsgu), (eg_ref, eu_ref, wgu))):
        for part, source in enumerate((gate, up)):
            pltpu.make_async_copy(
                source,
                both.at[:, :, pl.ds(part * hidden_units, hidden_units)],
                w_sem.at[1 + at],
            ).start()
    for at, (down, kept) in enumerate(((sd_ref, wsd), (ed_ref, wed))):
        for piece in range(2 * TP):
            pltpu.make_async_copy(
                down.at[:, pl.ds(piece * wide, wide)],
                kept.at[piece // 2, pl.ds((piece % 2) * hidden_units, hidden_units)],
                w_sem.at[3 + at],
            ).start()

    def arrived_weights(ref, at):
        pltpu.make_async_copy(ref, ref, w_sem.at[at]).wait()

    barrier = pltpu.get_barrier_semaphore()

    @pl.loop(1, groups)
    def _(step):
        pl.semaphore_signal(
            barrier,
            inc=1,
            device_id=(lax.rem(dp + step, groups), tp),
            device_id_type=MESH,
        )

    for neighbour in (left, right):
        pl.semaphore_signal(barrier, inc=1, device_id=(dp, neighbour), device_id_type=MESH)

    length = length_ref[0]
    live = lax.broadcasted_iota(jnp.int32, (window, rows), 1) < length
    expert_at = lax.broadcasted_iota(jnp.int32, (window, rows), 0)
    named = jnp.zeros((window, rows), F32)
    scale = jnp.zeros((window, rows), F32)
    for k in range(top):
        match = routes_ref[pl.ds(k, 1), :] == expert_at
        named = named + jnp.where(match, 1.0, 0.0)
        scale = scale + jnp.where(match, weights_ref[pl.ds(k, 1), :], 0.0)
    named = jnp.where(live, named, 0.0)
    before = jnp.where(
        lax.broadcasted_iota(jnp.int32, (rows, rows), 0)
        < lax.broadcasted_iota(jnp.int32, (rows, rows), 1),
        1.0,
        0.0,
    ).astype(BF16)
    place = jnp.where(named > 0.0, dot(named.astype(BF16), before), -1.0)
    group_of, _, _ = slot_parts((packed, window), 0)
    spread = jnp.where(placement_ref[...] == group_of, 1.0, 0.0).astype(BF16)
    _, half_of, want = slot_parts((packed, rows), 0)
    hit = dot(spread, place.astype(BF16)) == want.astype(F32)
    for half in range(2):
        sel[:, pl.ds(half * rows, rows)] = jnp.where(
            hit, jnp.where(half_of == half, 1.0, 0.0), 0.0
        ).astype(BF16)

    pl.semaphore_wait(barrier, groups - 1 + 2)

    def to(src, dst, send, recv, device):
        return pltpu.make_async_remote_copy(
            src_ref=src,
            dst_ref=dst,
            send_sem=send,
            recv_sem=recv,
            device_id=device,
            device_id_type=MESH,
        )

    arrived_weights(held.at[0], 0)

    def half_block(slot, half):
        return held.at[slot, pl.ds(half * rows, rows)]

    gathers = []
    for at, (source, half, target, landing, device) in enumerate(
        (
            (0, 0, 1, 0, right),
            (0, 1, 1, 1, left),
            (0, 1, 2, 0, right),
            (0, 0, 2, 1, left),
            (1, 0, 3, 0, right),
            (1, 1, 3, 1, left),
        )
    ):
        gathers.append(
            to(
                half_block(source, half),
                half_block(target, landing),
                ag_send.at[at],
                ag_recv.at[at],
                (dp, device),
            )
        )
    for at in range(2):
        gathers[at].start()

    my_chunk = dp // per_chunk

    def chunk_at(k):
        return lax.rem(my_chunk + k, CHUNKS)

    def send_chunk(source, landing, chunk, send, recv, local):
        @pl.loop(0, per_chunk)
        def _(step):
            target = chunk * per_chunk + lax.rem(dp + step, per_chunk)

            @pl.when(target != dp)
            def _():
                to(source.at[target], landing.at[dp], send, recv, (target, tp)).start()

            @pl.when(target == dp)
            def _():
                pltpu.make_async_copy(source.at[dp], landing.at[dp], local).start()

    def wait_peers(ref, sem, number):
        view = ref.at[pl.ds(0, number)]
        pltpu.make_async_copy(view, view, sem).wait()

    def from_chunk(k):
        return lax.rem(my_chunk + CHUNKS - k, CHUNKS)

    def wait_chunk(ref, k, recv, local):
        wait_peers(ref, recv.at[k], per_chunk - 1 if k == 0 else per_chunk)
        if k == 0:
            wait_peers(ref, local, 1)

    def select(slot):
        @pl.loop(0, CHUNKS)
        def _(k):
            chunk = chunk_at(k)
            picked = dot(
                sel[pl.ds(pl.multiple_of(chunk * chunk_rows, chunk_rows), chunk_rows), :],
                held[slot],
            )
            outgoing[slot, pl.ds(chunk * per_chunk, per_chunk)] = picked.reshape(
                per_chunk, 2 * MOST_R, wide
            ).astype(BF16)
            send_chunk(
                outgoing.at[slot],
                arrived.at[slot],
                chunk,
                d_send.at[slot],
                d_recv.at[slot, k],
                d_loc.at[slot],
            )

    def shared_step(slot):
        first, second = pieces[slot]
        total = dot(held[slot, pl.ds(0, rows)], wsgu[first]) + dot(
            held[slot, pl.ds(rows, rows)], wsgu[second]
        )
        if slot == 0:
            shared_acc[...] = total
        else:
            shared_acc[...] += total

    def load_chunk(ref, k):
        return ref[pl.ds(k * per_chunk, per_chunk)].astype(F32).reshape(chunk_rows, wide)

    def rows_of(chunk):
        return pl.ds(pl.multiple_of(chunk * chunk_rows, chunk_rows), chunk_rows)

    select(0)
    arrived_weights(wsgu, 1)
    shared_step(0)

    place = jnp.transpose(place).astype(BF16)
    scale = jnp.transpose(scale)
    head = scale.astype(BF16)
    rest = (scale - head.astype(F32)).astype(BF16)
    placement_col = jnp.transpose(
        jnp.broadcast_to(placement_ref[...].astype(F32), (8, window))
    )[:, :1]
    for chunk in range(CHUNKS):
        group_of, _, _ = slot_parts((window, chunk_rows), 1)
        group_of = (group_of + chunk * per_chunk).astype(F32)
        spread = jnp.where(placement_col == group_of, 1.0, 0.0).astype(BF16)
        _, half_of, want = slot_parts((rows, chunk_rows), 1)
        hit = dot(place, spread) == want.astype(F32)
        for part, kept in ((head, back_hi), (rest, back_lo)):
            value = jnp.where(hit, dot(part, spread), 0.0)
            for half in range(2):
                kept[chunk, pl.ds(half * rows, rows), :] = jnp.where(
                    half_of == half, value, 0.0
                ).astype(BF16)

    for at in (0, 1):
        gathers[at].wait_recv()
        gathers[at + 2].start()
        gathers[at + 4].start()
    select(1)
    shared_step(1)
    for slot in (2, 3):
        for at in (0, 1):
            gathers[2 * slot - 2 + at].wait_recv()
        select(slot)
        shared_step(slot)

    shared_hidden = (
        silu(shared_acc[:, pl.ds(0, hidden_units)])
        * shared_acc[:, pl.ds(hidden_units, hidden_units)]
    ).astype(BF16)
    arrived_weights(wsd, 3)
    for at, owner in ((0, across), (1, right), (2, left), (3, tp)):
        for half in range(2):
            part = dot(shared_hidden, wsd[owner, pl.ds(half * hidden_units, hidden_units)])
            if at < 3:
                s_part[at, pl.ds(half * rows, rows)] = part.astype(BF16)
            else:
                s_own[pl.ds(half * rows, rows)] = part

    def s_copy(at, part, half, landing, device):
        where = pl.ds(half * rows, rows)
        return to(
            s_part.at[part, where],
            landing.at[where],
            s_send.at[at],
            s_recv.at[at],
            (dp, device),
        )

    shared_sends = [
        s_copy(0, 0, 0, s_relay, right),
        s_copy(1, 0, 1, s_relay, left),
        s_copy(2, 1, 1, s_left, right),
        s_copy(3, 2, 0, s_right, left),
        s_copy(4, 1, 0, s_left, right),
        s_copy(5, 2, 1, s_right, left),
    ]
    for at in range(2):
        shared_sends[at].start()

    both = 2 * hidden_units

    def expert_chunk(slot, k):
        wait_chunk(arrived.at[slot], k, d_recv.at[slot], d_loc.at[slot])
        chunk = from_chunk(k)
        block = load_chunk(arrived.at[slot], chunk).astype(BF16)
        for half in range(2):
            where = (rows_of(chunk), pl.ds(half * both, both))
            total = dot(block, wgu[pieces[slot][half]])
            if slot == 0:
                acc[where] = total
            else:
                acc[where] += total

    def activate(chunk):
        first = acc[rows_of(chunk), pl.ds(0, both)]
        second = acc[rows_of(chunk), pl.ds(both, both)]
        total = first + pltpu.roll(second, chunk_rows - MOST_R, 0)
        inner = silu(total[:, :hidden_units]) * total[:, hidden_units:]
        _, half_of, _ = slot_parts((chunk_rows, hidden_units), 0)
        hid2[rows_of(chunk), pl.ds(0, hidden_units)] = jnp.where(
            half_of == 0, inner, 0.0
        ).astype(BF16)
        hid2[rows_of(chunk), pl.ds(hidden_units, hidden_units)] = jnp.where(
            half_of == 1, pltpu.roll(inner, MOST_R, 0), 0.0
        ).astype(BF16)

    def down(slot, owner, k):
        chunk = from_chunk(k)
        part = dot(hid2[rows_of(chunk), :], wed[owner])
        if slot is not None:
            outgoing[slot, pl.ds(chunk * per_chunk, per_chunk)] = part.reshape(
                per_chunk, 2 * MOST_R, wide
            ).astype(BF16)
        else:
            acc[rows_of(chunk), pl.ds(0, wide)] = part

    def e_copy(at, slot, k, landing, device):
        where = pl.ds(from_chunk(k) * per_chunk, per_chunk)
        return to(
            outgoing.at[slot, where],
            landing.at[where],
            e_send.at[at],
            e_recv.at[at],
            (dp, device),
        )

    relays, directs, passed = [], [], []
    for k in range(CHUNKS):
        ahead, behind = ((1, right, e_left), (2, left, e_right))[:: 1 if k % 2 == 0 else -1]
        relays.append(e_copy(k, 0, k, e_relay, ahead[1]))
        directs.append(e_copy(4 + k, behind[0], k, behind[2], behind[1]))
        passed.append((ahead, e_copy(8 + k, ahead[0], k, ahead[2], ahead[1])))

    def pass_on(k):
        (slot, _, _), copy = passed[k]
        where = pl.ds(from_chunk(k) * per_chunk, per_chunk)
        relays[k].wait_recv()
        outgoing[slot, where] = (
            outgoing[slot, where].astype(F32) + e_relay[where].astype(F32)
        ).astype(BF16)
        copy.start()

    def finish(k):
        chunk = from_chunk(k)
        down(None, tp, k)
        directs[k].wait_recv()
        passed[k][1].wait_recv()
        total = (
            acc[rows_of(chunk), pl.ds(0, wide)]
            + load_chunk(e_left, chunk)
            + load_chunk(e_right, chunk)
        )
        outgoing[3, pl.ds(chunk * per_chunk, per_chunk)] = total.reshape(
            per_chunk, 2 * MOST_R, wide
        ).astype(BF16)
        send_chunk(outgoing.at[3], came, chunk, c_send.at[0], c_recv.at[k], c_loc.at[0])

    arrived_weights(wgu, 2)
    for k in range(CHUNKS):
        expert_chunk(0, k)
    for at in (2, 3):
        shared_sends[at].start()
    for k in range(CHUNKS):
        expert_chunk(1, k)
    for at, part, half in ((0, 1, 0), (1, 2, 1)):
        shared_sends[at].wait_recv()
        where = pl.ds(half * rows, rows)
        s_part[part, where] = (
            s_part[part, where].astype(F32) + s_relay[where].astype(F32)
        ).astype(BF16)
        shared_sends[at + 4].start()
    for k in range(CHUNKS):
        expert_chunk(2, k)
    arrived_weights(wed, 4)
    for slot in range(3):
        wait_peers(outgoing.at[slot], d_send.at[slot], groups - 1)
    for k in range(CHUNKS):
        expert_chunk(3, k)
        activate(from_chunk(k))
        down(0, across, k)
        relays[k].start()
        slot, device = ((2, left), (1, right))[k % 2]
        down(slot, device, k)
        directs[k].start()
        (slot, device, _), _ = passed[k]
        down(slot, device, k)
        if k:
            pass_on(k - 1)
    pass_on(CHUNKS - 1)
    for at in range(2, 6):
        shared_sends[at].wait_recv()
    s_own[...] = s_own[...] + s_left[...].astype(F32) + s_right[...].astype(F32)
    wait_peers(outgoing.at[3], d_send.at[3], groups - 1)
    for k in range(CHUNKS):
        finish(k)

    for k in range(CHUNKS):
        wait_chunk(came, k, c_recv, c_loc.at[0])
        chunk = chunk_at(k)
        block = load_chunk(came, chunk).astype(BF16)
        s_own[...] += dot(back_hi[chunk], block) + dot(back_lo[chunk], block)
    keep = lax.broadcasted_iota(jnp.int32, (rows, wide), 0) < length
    for half in range(2):
        out_ref[:, pl.ds(half * wide, wide)] = jnp.where(
            keep, s_own[pl.ds(half * rows, rows)], 0.0
        ).astype(out_ref.dtype)

    for copy in gathers + shared_sends + relays + directs + [copy for _, copy in passed]:
        copy.wait_send()
    wait_peers(outgoing.at[3], c_send.at[0], groups - 1)


def local(
    hidden_in,
    lengths,
    routes,
    route_weights,
    placement,
    shared_gate,
    shared_up,
    shared_down,
    expert_gate,
    expert_up,
    expert_down,
):
    groups = lax.axis_size("dp")
    rows, quarter = hidden_in.shape
    wide = quarter // 2
    pieces = 2 * TP
    units = shared_gate.shape[1]
    window = placement.shape[0]
    packed = groups * 2 * MOST_R
    across_peers = (groups, 2 * MOST_R, wide)
    vmem = pl.BlockSpec(memory_space=pltpu.VMEM)
    smem = pl.BlockSpec(memory_space=pltpu.SMEM)
    hbm = pl.BlockSpec(memory_space=pl.ANY)
    dma = pltpu.SemaphoreType.DMA
    return pl.pallas_call(
        functools.partial(kernel, groups),
        out_shape=jax.ShapeDtypeStruct((rows, quarter), BF16),
        in_specs=[vmem] * 3 + [smem] + [hbm] * 7,
        out_specs=vmem,
        scratch_shapes=[
            pltpu.VMEM((pieces, wide, 2 * units), BF16),
            pltpu.VMEM((TP, 2 * units, wide), BF16),
            pltpu.VMEM((pieces, wide, 2 * units), BF16),
            pltpu.VMEM((TP, 2 * units, wide), BF16),
            pltpu.VMEM((TP, 2 * rows, wide), BF16),
            pltpu.VMEM((packed, 2 * rows), BF16),
            pltpu.VMEM((CHUNKS, 2 * rows, packed // CHUNKS), BF16),
            pltpu.VMEM((CHUNKS, 2 * rows, packed // CHUNKS), BF16),
            pltpu.VMEM((TP,) + across_peers, BF16),
            pltpu.VMEM((TP,) + across_peers, BF16),
            pltpu.VMEM((packed, 4 * units), F32),
            pltpu.VMEM((rows, 2 * units), F32),
            pltpu.VMEM((packed, 2 * units), BF16),
            pltpu.VMEM((3, 2 * rows, wide), BF16),
            pltpu.VMEM((2 * rows, wide), F32),
            pltpu.VMEM((2 * rows, wide), BF16),
            pltpu.VMEM((2 * rows, wide), BF16),
            pltpu.VMEM((2 * rows, wide), BF16),
            pltpu.VMEM(across_peers, BF16),
            pltpu.VMEM(across_peers, BF16),
            pltpu.VMEM(across_peers, BF16),
            pltpu.VMEM(across_peers, BF16),
            dma((5,)),
            dma((6,)),
            dma((6,)),
            dma((TP,)),
            dma((TP, CHUNKS)),
            dma((TP,)),
            dma((6,)),
            dma((6,)),
            dma((12,)),
            dma((12,)),
            dma((1,)),
            dma((CHUNKS,)),
            dma((1,)),
        ],
        compiler_params=pltpu.CompilerParams(
            collective_id=0, has_side_effects=True, vmem_limit_bytes=62 << 20
        ),
        cost_estimate=pl.CostEstimate(
            flops=2 * 5 * rows * quarter * 4 * units * 3 // 2,
            bytes_accessed=6 * quarter * 4 * units * 2,
            transcendentals=0,
        ),
    )(
        routes.T,
        route_weights.T,
        placement.reshape(1, window),
        lengths,
        hidden_in,
        shared_gate.reshape(pieces, wide, units),
        shared_up.reshape(pieces, wide, units),
        shared_down,
        expert_gate.reshape(pieces, wide, units),
        expert_up.reshape(pieces, wide, units),
        expert_down[0],
    )


def solution(mesh):
    in_specs = (
        P("dp", "tp"),
        P("dp"),
        P("dp", None),
        P("dp", None),
        P(),
        P(None, "tp"),
        P(None, "tp"),
        P("tp", None),
        P("dp", None, "tp"),
        P("dp", None, "tp"),
        P("dp", "tp", None),
    )
    out_specs = P("dp", "tp")
    return jax.shard_map(local, mesh=mesh, in_specs=in_specs, out_specs=out_specs, check_vma=False)
```

```python
import functools
import math

import jax
import jax.numpy as jnp
from jax import lax
from jax.experimental import pallas as pl
from jax.experimental.pallas import tpu as pltpu
from jax.sharding import PartitionSpec as P

MOST_R = 12
MESH = pl.DeviceIdType.MESH
BF16 = jnp.bfloat16
F32 = jnp.float32
TP = 4
WINDOW = 4


def dot(a, b):
    return jnp.dot(a, b, preferred_element_type=F32)


def silu(v):
    return v / (1.0 + jnp.exp(-v))


def slot_parts(shape, axis):
    at = lax.broadcasted_iota(jnp.int32, shape, axis)
    group = (at * 2731) >> 16
    place = at - group * (2 * MOST_R)
    half = (place >= MOST_R).astype(jnp.int32)
    return group, half, place - MOST_R * half


def side_of(groups):
    side = math.isqrt(groups // 2)
    assert 2 * side * side == groups and side & (side - 1) == 0
    return side


def device_at(place, side):
    bits = side.bit_length() - 1
    chunk = place >> (bits + 1)
    x = (place >> 1) & (side - 1)
    z = (chunk + side - x) & (side - 1)
    return 2 * (side * x + z) + (place & 1)


def kernel(
    groups,
    routes_ref,
    weights_ref,
    placement_ref,
    length_ref,
    hidden_ref,
    sg_ref,
    su_ref,
    sd_ref,
    eg_ref,
    eu_ref,
    ed_ref,
    out_ref,
    wsgu,
    wsd,
    wgu,
    wed,
    held,
    sel,
    back_hi,
    back_lo,
    outgoing,
    arrived,
    acc,
    shared_acc,
    hid2,
    s_hidden,
    s_own,
    others,
    e_relay,
    e_left,
    e_right,
    came,
    w_sem,
    ag_send,
    ag_recv,
    d_send,
    d_recv,
    d_loc,
    s_send,
    s_recv,
    p_sem,
    e_send,
    e_recv,
    c_send,
    c_recv,
    c_loc,
):
    dp = lax.axis_index("dp")
    tp = lax.axis_index("tp")
    right = lax.rem(tp + 1, TP)
    left = lax.rem(tp + TP - 1, TP)
    across = lax.rem(tp + 2, TP)
    rows = held.shape[1] // 2
    wide = held.shape[2]
    window = placement_ref.shape[1]
    chunks = side_of(groups)
    hidden_units = ed_ref.shape[0]
    per_chunk = groups // chunks
    chunk_rows = per_chunk * 2 * MOST_R
    packed = groups * 2 * MOST_R
    top = routes_ref.shape[0]
    pieces = (
        (2 * tp, 2 * tp + 1),
        (2 * left, 2 * right + 1),
        (2 * left + 1, 2 * right),
        (2 * across, 2 * across + 1),
    )

    for half in range(2):
        pltpu.make_async_copy(
            hidden_ref.at[:, pl.ds(half * wide, wide)],
            held.at[0, pl.ds(half * rows, rows)],
            w_sem.at[0],
        ).start()
    for at, (gate, up, both) in enumerate(((sg_ref, su_ref, wsgu), (eg_ref, eu_ref, wgu))):
        for part, source in enumerate((gate, up)):
            pltpu.make_async_copy(
                source,
                both.at[:, :, pl.ds(part * hidden_units, hidden_units)],
                w_sem.at[1 + at],
            ).start()
    def columns(piece):
        return pl.ds(pl.multiple_of(piece * wide, wide), wide)

    for half in range(2):
        pltpu.make_async_copy(
            sd_ref.at[:, columns(2 * tp + half)], wsd.at[half], w_sem.at[3]
        ).start()
    for piece in range(2 * TP):
        pltpu.make_async_copy(
            ed_ref.at[:, pl.ds(piece * wide, wide)],
            wed.at[piece // 2, pl.ds((piece % 2) * hidden_units, hidden_units)],
            w_sem.at[4],
        ).start()

    def arrived_weights(ref, at):
        pltpu.make_async_copy(ref, ref, w_sem.at[at]).wait()

    barrier = pltpu.get_barrier_semaphore()

    @pl.loop(1, groups)
    def _(step):
        pl.semaphore_signal(
            barrier,
            inc=1,
            device_id=(lax.rem(dp + step, groups), tp),
            device_id_type=MESH,
        )

    for neighbour in (left, right, across):
        pl.semaphore_signal(barrier, inc=1, device_id=(dp, neighbour), device_id_type=MESH)

    length = length_ref[0]
    live = lax.broadcasted_iota(jnp.int32, (window, rows), 1) < length
    expert_at = lax.broadcasted_iota(jnp.int32, (window, rows), 0)
    named = jnp.zeros((window, rows), F32)
    scale = jnp.zeros((window, rows), F32)
    for k in range(top):
        match = routes_ref[pl.ds(k, 1), :] == expert_at
        named = named + jnp.where(match, 1.0, 0.0)
        scale = scale + jnp.where(match, weights_ref[pl.ds(k, 1), :], 0.0)
    named = jnp.where(live, named, 0.0)
    before = jnp.where(
        lax.broadcasted_iota(jnp.int32, (rows, rows), 0)
        < lax.broadcasted_iota(jnp.int32, (rows, rows), 1),
        1.0,
        0.0,
    ).astype(BF16)
    place = jnp.where(named > 0.0, dot(named.astype(BF16), before), -1.0)
    group_of, _, _ = slot_parts((packed, window), 0)
    spread = jnp.where(placement_ref[...] == device_at(group_of, chunks), 1.0, 0.0).astype(BF16)
    _, half_of, want = slot_parts((packed, rows), 0)
    hit = dot(spread, place.astype(BF16)) == want.astype(F32)
    for half in range(2):
        sel[:, pl.ds(half * rows, rows)] = jnp.where(
            hit, jnp.where(half_of == half, 1.0, 0.0), 0.0
        ).astype(BF16)

    pl.semaphore_wait(barrier, groups - 1 + 3)

    def to(src, dst, send, recv, device):
        return pltpu.make_async_remote_copy(
            src_ref=src,
            dst_ref=dst,
            send_sem=send,
            recv_sem=recv,
            device_id=device,
            device_id_type=MESH,
        )

    arrived_weights(held.at[0], 0)

    def half_block(slot, half):
        return held.at[slot, pl.ds(half * rows, rows)]

    gathers = []
    for at, (source, half, target, landing, device) in enumerate(
        (
            (0, 0, 1, 0, right),
            (0, 1, 1, 1, left),
            (0, 1, 2, 0, right),
            (0, 0, 2, 1, left),
            (1, 0, 3, 0, right),
            (1, 1, 3, 1, left),
        )
    ):
        gathers.append(
            to(
                half_block(source, half),
                half_block(target, landing),
                ag_send.at[at],
                ag_recv.at[at],
                (dp, device),
            )
        )
    for at in range(2):
        gathers[at].start()

    chips = groups // 2
    chip, core = dp // 2, lax.rem(dp, 2)
    share = others.shape[3]

    fetches = [
        to(
            sd_ref.at[pl.ds(pl.multiple_of(chip * share, share), share), columns(2 * device + core)],
            others.at[core, chip, place],
            s_send.at[at],
            s_recv.at[at],
            (dp, device),
        )
        for at, (device, place) in enumerate(((right, 2), (left, 0), (across, 1)))
    ]
    for copy in fetches:
        copy.start()

    my_x = dp // per_chunk
    my_chunk = lax.rem(my_x + lax.rem(dp // 2, chunks), chunks)
    my_place_in = 2 * my_x + lax.rem(dp, 2)
    me = my_chunk * per_chunk + my_place_in

    def rows_of(chunk):
        return pl.ds(pl.multiple_of(chunk * chunk_rows, chunk_rows), chunk_rows)

    def chunk_at(k):
        return lax.rem(my_chunk + k, chunks)

    def send_chunk(source, landing, chunk, send, recv, local):
        @pl.loop(0, per_chunk)
        def _(step):
            place = lax.rem(my_place_in + step, per_chunk)
            x = place // 2
            device = 2 * (chunks * x + lax.rem(chunk + chunks - x, chunks)) + lax.rem(place, 2)
            there = chunk * per_chunk + place

            @pl.when(device != dp)
            def _():
                to(source.at[there], landing.at[me], send, recv, (device, tp)).start()

            @pl.when(device == dp)
            def _():
                pltpu.make_async_copy(source.at[me], landing.at[me], local).start()

    def wait_peers(ref, sem, number):
        view = ref.at[pl.ds(0, number)]
        pltpu.make_async_copy(view, view, sem).wait()

    def from_chunk(k):
        return lax.rem(my_chunk + chunks - k, chunks)

    def wait_chunk(ref, k, recv, local):
        wait_peers(ref, recv.at[k], per_chunk - 1 if k == 0 else per_chunk)
        if k == 0:
            wait_peers(ref, local, 1)

    def issue(slot, k):
        send_chunk(
            outgoing.at[slot],
            arrived.at[slot],
            chunk_at(k),
            d_send.at[slot, k],
            d_recv.at[slot, k],
            d_loc.at[slot],
        )

    def wait_issued(slot, k):
        wait_peers(outgoing.at[slot], d_send.at[slot, k], per_chunk - (k == 0))

    def issue_next(slot, *ks):
        for k in ks:
            earlier = slot * chunks + k - WINDOW
            if earlier >= 0:
                wait_issued(earlier // chunks, earlier % chunks)
            issue(slot, k)

    def select(slot):
        @pl.loop(0, chunks)
        def _(k):
            chunk = chunk_at(k)
            picked = dot(sel[rows_of(chunk), :], held[slot])
            outgoing[slot, pl.ds(chunk * per_chunk, per_chunk)] = picked.reshape(
                per_chunk, 2 * MOST_R, wide
            ).astype(BF16)
            if slot == 0:
                issue(slot, k)

    def shared_step(slot):
        first, second = pieces[slot]
        total = dot(held[slot, pl.ds(0, rows)], wsgu[first]) + dot(
            held[slot, pl.ds(rows, rows)], wsgu[second]
        )
        if slot == 0:
            shared_acc[...] = total
        else:
            shared_acc[...] += total

    def load_chunk(ref, k):
        return ref[pl.ds(k * per_chunk, per_chunk)].astype(F32).reshape(chunk_rows, wide)

    select(0)
    arrived_weights(wsgu, 1)
    shared_step(0)

    place = jnp.transpose(place).astype(BF16)
    scale = jnp.transpose(scale)
    head = scale.astype(BF16)
    rest = (scale - head.astype(F32)).astype(BF16)
    placement_col = jnp.transpose(
        jnp.broadcast_to(placement_ref[...].astype(F32), (8, window))
    )[:, :1]
    for chunk in range(chunks):
        group_of, _, _ = slot_parts((window, chunk_rows), 1)
        group_of = device_at(group_of + chunk * per_chunk, chunks).astype(F32)
        spread = jnp.where(placement_col == group_of, 1.0, 0.0).astype(BF16)
        _, half_of, want = slot_parts((rows, chunk_rows), 1)
        hit = dot(place, spread) == want.astype(F32)
        for part, kept in ((head, back_hi), (rest, back_lo)):
            value = jnp.where(hit, dot(part, spread), 0.0)
            for half in range(2):
                kept[chunk, pl.ds(half * rows, rows), :] = jnp.where(
                    half_of == half, value, 0.0
                ).astype(BF16)

    both = 2 * hidden_units

    def expert_chunk(slot, k):
        wait_chunk(arrived.at[slot], k, d_recv.at[slot], d_loc.at[slot])
        chunk = from_chunk(k)
        block = load_chunk(arrived.at[slot], chunk).astype(BF16)
        for half in range(2):
            where = (rows_of(chunk), pl.ds(half * both, both))
            total = dot(block, wgu[pieces[slot][half]])
            if slot == 0:
                acc[where] = total
            else:
                acc[where] += total

    def activate(chunk):
        first = acc[rows_of(chunk), pl.ds(0, both)]
        second = acc[rows_of(chunk), pl.ds(both, both)]
        total = first + pltpu.roll(second, chunk_rows - MOST_R, 0)
        inner = silu(total[:, :hidden_units]) * total[:, hidden_units:]
        _, half_of, _ = slot_parts((chunk_rows, hidden_units), 0)
        hid2[rows_of(chunk), pl.ds(0, hidden_units)] = jnp.where(
            half_of == 0, inner, 0.0
        ).astype(BF16)
        hid2[rows_of(chunk), pl.ds(hidden_units, hidden_units)] = jnp.where(
            half_of == 1, pltpu.roll(inner, MOST_R, 0), 0.0
        ).astype(BF16)

    def down(slot, owner, k):
        chunk = from_chunk(k)
        part = dot(hid2[rows_of(chunk), :], wed[owner])
        if slot is not None:
            outgoing[slot, pl.ds(chunk * per_chunk, per_chunk)] = part.reshape(
                per_chunk, 2 * MOST_R, wide
            ).astype(BF16)
        else:
            acc[rows_of(chunk), pl.ds(0, wide)] = part

    def e_copy(at, slot, k, landing, device):
        where = pl.ds(from_chunk(k) * per_chunk, per_chunk)
        return to(
            outgoing.at[slot, where],
            landing.at[where],
            e_send.at[at],
            e_recv.at[at],
            (dp, device),
        )

    relays, directs, passed = [], [], []
    for k in range(chunks):
        ahead, behind = ((1, right, e_left), (2, left, e_right))[:: 1 if k % 2 == 0 else -1]
        relays.append(e_copy(k, 0, k, e_relay, ahead[1]))
        directs.append(e_copy(4 + k, behind[0], k, behind[2], behind[1]))
        passed.append((ahead, e_copy(8 + k, ahead[0], k, ahead[2], ahead[1])))

    def pass_on(k):
        (slot, _, _), copy = passed[k]
        where = pl.ds(from_chunk(k) * per_chunk, per_chunk)
        relays[k].wait_recv()
        outgoing[slot, where] = (
            outgoing[slot, where].astype(F32) + e_relay[where].astype(F32)
        ).astype(BF16)
        copy.start()

    def finish(k):
        chunk = from_chunk(k)
        directs[k].wait_recv()
        passed[k][1].wait_recv()
        total = (
            acc[rows_of(chunk), pl.ds(0, wide)]
            + load_chunk(e_left, chunk)
            + load_chunk(e_right, chunk)
        )
        outgoing[3, pl.ds(chunk * per_chunk, per_chunk)] = total.reshape(
            per_chunk, 2 * MOST_R, wide
        ).astype(BF16)
        send_chunk(outgoing.at[3], came, chunk, c_send.at[0], c_recv.at[k], c_loc.at[0])

    first, second = range(chunks // 2), range(chunks // 2, chunks)
    for at in (0, 1):
        gathers[at].wait_recv()
        gathers[at + 2].start()
        gathers[at + 4].start()
    select(1)
    for k in range(chunks - WINDOW):
        wait_issued(0, k)
    issue_next(1, *first)
    arrived_weights(wgu, 2)
    for k in range(chunks):
        expert_chunk(0, k)
    issue_next(1, *second)
    shared_step(1)
    for k in first:
        expert_chunk(1, k)
    for at in (2, 3):
        gathers[at].wait_recv()
    select(2)
    issue_next(2, *first)
    for at in (4, 5):
        gathers[at].wait_recv()
    select(3)
    shared_step(2)
    shared_step(3)

    shared_hidden = (
        silu(shared_acc[:, pl.ds(0, hidden_units)])
        * shared_acc[:, pl.ds(hidden_units, hidden_units)]
    ).astype(BF16)
    s_hidden[0] = shared_hidden
    hidden_sends = [
        to(
            s_hidden.at[0],
            s_hidden.at[place],
            s_send.at[3 + at],
            s_recv.at[3 + at],
            (dp, device),
        )
        for at, (device, place) in enumerate(((right, 3), (left, 1), (across, 2)))
    ]
    for copy in hidden_sends:
        copy.start()

    issue_next(2, *second)
    for k in second:
        expert_chunk(1, k)
    issue_next(3, *first)
    for k in first:
        expert_chunk(2, k)
    issue_next(3, *second)

    for copy in fetches:
        copy.wait_recv()

    @pl.loop(1, chips)
    def _(step):
        target = 2 * lax.rem(chip + step, chips) + core
        to(
            others.at[core, chip],
            others.at[core, chip],
            p_sem.at[0],
            p_sem.at[1],
            (target, tp),
        ).start()

    for k in second:
        expert_chunk(2, k)
    arrived_weights(wed, 4)
    for k in range(chunks):
        expert_chunk(3, k)
        activate(from_chunk(k))
        down(0, across, k)
        if k in first:
            relays[k].start()
        slot, device = ((2, left), (1, right))[k % 2]
        down(slot, device, k)
        if k in first:
            directs[k].start()
        (slot, device, _), _ = passed[k]
        down(slot, device, k)
        down(None, tp, k)
    for k in first:
        pass_on(k)
    for k in second:
        relays[k].start()
    for at in range(WINDOW):
        wait_issued(3, chunks - 1 - at)
    for k in first:
        finish(k)
    for k in second:
        directs[k].start()
    for k in second:
        pass_on(k)
    wait_peers(others.at[core], p_sem.at[1], chips - 1)
    swap = to(
        others.at[core], others.at[core], p_sem.at[2], p_sem.at[3], (dp + 1 - 2 * core, tp)
    )
    swap.start()
    for k in second:
        finish(k)

    for copy in hidden_sends:
        copy.wait_recv()
    arrived_weights(wsd, 3)
    swap.wait_recv()
    for half in range(2):
        total = dot(s_hidden[0], wsd[half])
        for place in range(TP - 1):
            total += dot(
                s_hidden[place + 1], others[half, :, place].reshape(hidden_units, wide)
            )
        s_own[pl.ds(half * rows, rows)] = total

    for k in range(chunks):
        wait_chunk(came, k, c_recv, c_loc.at[0])
        chunk = chunk_at(k)
        block = load_chunk(came, chunk).astype(BF16)
        s_own[...] += dot(back_hi[chunk], block) + dot(back_lo[chunk], block)
    keep = lax.broadcasted_iota(jnp.int32, (rows, wide), 0) < length
    for half in range(2):
        out_ref[:, pl.ds(half * wide, wide)] = jnp.where(
            keep, s_own[pl.ds(half * rows, rows)], 0.0
        ).astype(out_ref.dtype)

    sends = gathers + fetches + hidden_sends + [swap]
    for copy in sends + relays + directs + [copy for _, copy in passed]:
        copy.wait_send()
    wait_peers(others.at[core], p_sem.at[0], chips - 1)
    wait_peers(outgoing.at[3], c_send.at[0], groups - 1)


def local(
    hidden_in,
    lengths,
    routes,
    route_weights,
    placement,
    shared_gate,
    shared_up,
    shared_down,
    expert_gate,
    expert_up,
    expert_down,
):
    groups = lax.axis_size("dp")
    rows, quarter = hidden_in.shape
    wide = quarter // 2
    pieces = 2 * TP
    units = shared_gate.shape[1]
    window = placement.shape[0]
    chunks = side_of(groups)
    packed = groups * 2 * MOST_R
    across_peers = (groups, 2 * MOST_R, wide)
    vmem = pl.BlockSpec(memory_space=pltpu.VMEM)
    smem = pl.BlockSpec(memory_space=pltpu.SMEM)
    hbm = pl.BlockSpec(memory_space=pl.ANY)
    dma = pltpu.SemaphoreType.DMA
    return pl.pallas_call(
        functools.partial(kernel, groups),
        out_shape=jax.ShapeDtypeStruct((rows, quarter), BF16),
        in_specs=[vmem] * 3 + [smem] + [hbm] * 7,
        out_specs=vmem,
        scratch_shapes=[
            pltpu.VMEM((pieces, wide, 2 * units), BF16),
            pltpu.VMEM((2, units, wide), BF16),
            pltpu.VMEM((pieces, wide, 2 * units), BF16),
            pltpu.VMEM((TP, 2 * units, wide), BF16),
            pltpu.VMEM((TP, 2 * rows, wide), BF16),
            pltpu.VMEM((packed, 2 * rows), BF16),
            pltpu.VMEM((chunks, 2 * rows, packed // chunks), BF16),
            pltpu.VMEM((chunks, 2 * rows, packed // chunks), BF16),
            pltpu.VMEM((TP,) + across_peers, BF16),
            pltpu.VMEM((TP,) + across_peers, BF16),
            pltpu.VMEM((packed, 4 * units), F32),
            pltpu.VMEM((rows, 2 * units), F32),
            pltpu.VMEM((packed, 2 * units), BF16),
            pltpu.VMEM((TP, rows, units), BF16),
            pltpu.VMEM((2 * rows, wide), F32),
            pltpu.VMEM((2, groups // 2, TP - 1, 2 * units // groups, wide), BF16),
            pltpu.VMEM(across_peers, BF16),
            pltpu.VMEM(across_peers, BF16),
            pltpu.VMEM(across_peers, BF16),
            pltpu.VMEM(across_peers, BF16),
            dma((5,)),
            dma((6,)),
            dma((6,)),
            dma((TP, chunks)),
            dma((TP, chunks)),
            dma((TP,)),
            dma((6,)),
            dma((6,)),
            dma((4,)),
            dma((12,)),
            dma((12,)),
            dma((1,)),
            dma((chunks,)),
            dma((1,)),
        ],
        compiler_params=pltpu.CompilerParams(
            collective_id=0, has_side_effects=True, vmem_limit_bytes=62 << 20
        ),
        cost_estimate=pl.CostEstimate(
            flops=2 * 5 * rows * quarter * 4 * units * 3 // 2,
            bytes_accessed=6 * quarter * 4 * units * 2,
            transcendentals=0,
        ),
    )(
        routes.T,
        route_weights.T,
        placement.reshape(1, window),
        lengths,
        hidden_in,
        shared_gate.reshape(pieces, wide, units),
        shared_up.reshape(pieces, wide, units),
        shared_down,
        expert_gate.reshape(pieces, wide, units),
        expert_up.reshape(pieces, wide, units),
        expert_down[0],
    )


def solution(mesh):
    in_specs = (
        P("dp", "tp"),
        P("dp"),
        P("dp", None),
        P("dp", None),
        P(),
        P(None, "tp"),
        P(None, "tp"),
        P("tp", None),
        P("dp", None, "tp"),
        P("dp", None, "tp"),
        P("dp", "tp", None),
    )
    out_specs = P("dp", "tp")
    return jax.shard_map(local, mesh=mesh, in_specs=in_specs, out_specs=out_specs, check_vma=False)
```

```python
import functools
import math

import jax
import jax.numpy as jnp
from jax import lax
from jax.experimental import pallas as pl
from jax.experimental.pallas import tpu as pltpu
from jax.sharding import PartitionSpec as P

MOST_R = 12
MESH = pl.DeviceIdType.MESH
BF16 = jnp.bfloat16
F32 = jnp.float32
TP = 4
WINDOW = 4


def dot(a, b):
    return jnp.dot(a, b, preferred_element_type=F32)


def silu(v):
    return v / (1.0 + jnp.exp(-v))


def slot_parts(shape, axis):
    at = lax.broadcasted_iota(jnp.int32, shape, axis)
    group = (at * 2731) >> 16
    place = at - group * (2 * MOST_R)
    half = (place >= MOST_R).astype(jnp.int32)
    return group, half, place - MOST_R * half


def side_of(groups):
    side = math.isqrt(groups // 2)
    assert 2 * side * side == groups and side & (side - 1) == 0
    return side


def device_at(place, side):
    bits = side.bit_length() - 1
    chunk = place >> (bits + 1)
    x = (place >> 1) & (side - 1)
    z = (chunk + side - x) & (side - 1)
    return 2 * (side * x + z) + (place & 1)


def kernel(
    groups,
    routes_ref,
    weights_ref,
    placement_ref,
    length_ref,
    hidden_ref,
    sg_ref,
    su_ref,
    sd_ref,
    eg_ref,
    eu_ref,
    ed_ref,
    out_ref,
    wsgu,
    wsd,
    wgu,
    wed,
    held,
    sel,
    back_hi,
    back_lo,
    outgoing,
    arrived,
    acc,
    shared_acc,
    hid2,
    s_hidden,
    s_own,
    others,
    for_left,
    e_relay,
    e_left,
    e_right,
    came,
    w_sem,
    ag_send,
    ag_recv,
    d_send,
    d_recv,
    d_loc,
    s_send,
    s_recv,
    p_sem,
    e_send,
    e_recv,
    c_send,
    c_recv,
    c_loc,
):
    dp = lax.axis_index("dp")
    tp = lax.axis_index("tp")
    right = lax.rem(tp + 1, TP)
    left = lax.rem(tp + TP - 1, TP)
    across = lax.rem(tp + 2, TP)
    rows = held.shape[1] // 2
    wide = held.shape[2]
    window = placement_ref.shape[1]
    chunks = side_of(groups)
    hidden_units = ed_ref.shape[0]
    per_chunk = groups // chunks
    chunk_rows = per_chunk * 2 * MOST_R
    packed = groups * 2 * MOST_R
    top = routes_ref.shape[0]
    pieces = (
        (2 * tp, 2 * tp + 1),
        (2 * left, 2 * right + 1),
        (2 * left + 1, 2 * right),
        (2 * across, 2 * across + 1),
    )

    for half in range(2):
        pltpu.make_async_copy(
            hidden_ref.at[:, pl.ds(half * wide, wide)],
            held.at[0, pl.ds(half * rows, rows)],
            w_sem.at[0],
        ).start()
    for at, (gate, up, both) in enumerate(((sg_ref, su_ref, wsgu), (eg_ref, eu_ref, wgu))):
        for part, source in enumerate((gate, up)):
            pltpu.make_async_copy(
                source,
                both.at[:, :, pl.ds(part * hidden_units, hidden_units)],
                w_sem.at[1 + at],
            ).start()
    def columns(piece):
        return pl.ds(pl.multiple_of(piece * wide, wide), wide)

    for half in range(2):
        pltpu.make_async_copy(
            sd_ref.at[:, columns(2 * tp + half)], wsd.at[half], w_sem.at[3]
        ).start()
    for piece in range(2 * TP):
        pltpu.make_async_copy(
            ed_ref.at[:, pl.ds(piece * wide, wide)],
            wed.at[piece // 2, pl.ds((piece % 2) * hidden_units, hidden_units)],
            w_sem.at[4],
        ).start()

    def arrived_weights(ref, at):
        pltpu.make_async_copy(ref, ref, w_sem.at[at]).wait()

    barrier = pltpu.get_barrier_semaphore()

    @pl.loop(1, groups)
    def _(step):
        pl.semaphore_signal(
            barrier,
            inc=1,
            device_id=(lax.rem(dp + step, groups), tp),
            device_id_type=MESH,
        )

    for neighbour in (left, right, across):
        pl.semaphore_signal(barrier, inc=1, device_id=(dp, neighbour), device_id_type=MESH)

    length = length_ref[0]
    live = lax.broadcasted_iota(jnp.int32, (window, rows), 1) < length
    expert_at = lax.broadcasted_iota(jnp.int32, (window, rows), 0)
    named = jnp.zeros((window, rows), F32)
    scale = jnp.zeros((window, rows), F32)
    for k in range(top):
        match = routes_ref[pl.ds(k, 1), :] == expert_at
        named = named + jnp.where(match, 1.0, 0.0)
        scale = scale + jnp.where(match, weights_ref[pl.ds(k, 1), :], 0.0)
    named = jnp.where(live, named, 0.0)
    before = jnp.where(
        lax.broadcasted_iota(jnp.int32, (rows, rows), 0)
        < lax.broadcasted_iota(jnp.int32, (rows, rows), 1),
        1.0,
        0.0,
    ).astype(BF16)
    place = jnp.where(named > 0.0, dot(named.astype(BF16), before), -1.0)
    group_of, _, _ = slot_parts((packed, window), 0)
    spread = jnp.where(placement_ref[...] == device_at(group_of, chunks), 1.0, 0.0).astype(BF16)
    _, half_of, want = slot_parts((packed, rows), 0)
    hit = dot(spread, place.astype(BF16)) == want.astype(F32)
    for half in range(2):
        sel[:, pl.ds(half * rows, rows)] = jnp.where(
            hit, jnp.where(half_of == half, 1.0, 0.0), 0.0
        ).astype(BF16)

    pl.semaphore_wait(barrier, groups - 1 + 3)

    def to(src, dst, send, recv, device):
        return pltpu.make_async_remote_copy(
            src_ref=src,
            dst_ref=dst,
            send_sem=send,
            recv_sem=recv,
            device_id=device,
            device_id_type=MESH,
        )

    arrived_weights(held.at[0], 0)

    def half_block(slot, half):
        return held.at[slot, pl.ds(half * rows, rows)]

    gathers = []
    for at, (source, half, target, landing, device) in enumerate(
        (
            (0, 0, 1, 0, right),
            (0, 1, 1, 1, left),
            (0, 1, 2, 0, right),
            (0, 0, 2, 1, left),
            (1, 0, 3, 0, right),
            (1, 1, 3, 1, left),
        )
    ):
        gathers.append(
            to(
                half_block(source, half),
                half_block(target, landing),
                ag_send.at[at],
                ag_recv.at[at],
                (dp, device),
            )
        )
    for at in range(2):
        gathers[at].start()

    chips = groups // 2
    chip, core = dp // 2, lax.rem(dp, 2)
    share = others.shape[3]

    fetches = [
        to(
            sd_ref.at[pl.ds(pl.multiple_of(chip * share, share), share), columns(2 * device + core)],
            others.at[core, chip, place],
            s_send.at[at],
            s_recv.at[at],
            (dp, device),
        )
        for at, (device, place) in enumerate(((right, 2), (left, 0), (across, 1)))
    ]
    for copy in fetches:
        copy.start()

    my_x = dp // per_chunk
    my_chunk = lax.rem(my_x + lax.rem(dp // 2, chunks), chunks)
    my_place_in = 2 * my_x + lax.rem(dp, 2)
    me = my_chunk * per_chunk + my_place_in

    def rows_of(chunk):
        return pl.ds(pl.multiple_of(chunk * chunk_rows, chunk_rows), chunk_rows)

    def chunk_at(k):
        return lax.rem(my_chunk + k, chunks)

    def send_chunk(source, landing, chunk, send, recv, local):
        @pl.loop(0, per_chunk)
        def _(step):
            place = lax.rem(my_place_in + step, per_chunk)
            x = place // 2
            device = 2 * (chunks * x + lax.rem(chunk + chunks - x, chunks)) + lax.rem(place, 2)
            there = chunk * per_chunk + place

            @pl.when(device != dp)
            def _():
                to(source.at[there], landing.at[me], send, recv, (device, tp)).start()

            @pl.when(device == dp)
            def _():
                pltpu.make_async_copy(source.at[me], landing.at[me], local).start()

    def wait_peers(ref, sem, number):
        view = ref.at[pl.ds(0, number)]
        pltpu.make_async_copy(view, view, sem).wait()

    def from_chunk(k):
        return lax.rem(my_chunk + chunks - k, chunks)

    def wait_chunk(ref, k, recv, local):
        wait_peers(ref, recv.at[k], per_chunk - 1 if k == 0 else per_chunk)
        if k == 0:
            wait_peers(ref, local, 1)

    def issue(slot, k):
        send_chunk(
            outgoing.at[slot],
            arrived.at[slot],
            chunk_at(k),
            d_send.at[slot, k],
            d_recv.at[slot, k],
            d_loc.at[slot],
        )

    def wait_issued(slot, k):
        wait_peers(outgoing.at[slot], d_send.at[slot, k], per_chunk - (k == 0))

    queue = [(0, k) for k in range(chunks)]
    waited = []

    def wait_queue(number):
        while len(waited) < number:
            wait_issued(*queue[len(waited)])
            waited.append(1)

    def issue_next(*which):
        for slot, k in which:
            wait_queue(len(queue) + 1 - WINDOW)
            issue(slot, k)
            queue.append((slot, k))

    def select(slot):
        @pl.loop(0, chunks)
        def _(k):
            chunk = chunk_at(k)
            picked = dot(sel[rows_of(chunk), :], held[slot])
            outgoing[slot, pl.ds(chunk * per_chunk, per_chunk)] = picked.reshape(
                per_chunk, 2 * MOST_R, wide
            ).astype(BF16)
            if slot == 0:
                issue(slot, k)

    def shared_step(slot):
        first, second = pieces[slot]
        total = dot(held[slot, pl.ds(0, rows)], wsgu[first]) + dot(
            held[slot, pl.ds(rows, rows)], wsgu[second]
        )
        if slot == 0:
            shared_acc[...] = total
        else:
            shared_acc[...] += total

    def load_chunk(ref, k):
        return ref[pl.ds(k * per_chunk, per_chunk)].astype(F32).reshape(chunk_rows, wide)

    select(0)
    arrived_weights(wsgu, 1)
    shared_step(0)

    place = jnp.transpose(place).astype(BF16)
    scale = jnp.transpose(scale)
    head = scale.astype(BF16)
    rest = (scale - head.astype(F32)).astype(BF16)
    placement_col = jnp.transpose(
        jnp.broadcast_to(placement_ref[...].astype(F32), (8, window))
    )[:, :1]
    for chunk in range(chunks):
        group_of, _, _ = slot_parts((window, chunk_rows), 1)
        group_of = device_at(group_of + chunk * per_chunk, chunks).astype(F32)
        spread = jnp.where(placement_col == group_of, 1.0, 0.0).astype(BF16)
        _, half_of, want = slot_parts((rows, chunk_rows), 1)
        hit = dot(place, spread) == want.astype(F32)
        for part, kept in ((head, back_hi), (rest, back_lo)):
            value = jnp.where(hit, dot(part, spread), 0.0)
            for half in range(2):
                kept[chunk, pl.ds(half * rows, rows), :] = jnp.where(
                    half_of == half, value, 0.0
                ).astype(BF16)

    both = 2 * hidden_units

    def expert_chunk(slot, k):
        wait_chunk(arrived.at[slot], k, d_recv.at[slot], d_loc.at[slot])
        chunk = from_chunk(k)
        block = load_chunk(arrived.at[slot], chunk).astype(BF16)
        for half in range(2):
            where = (rows_of(chunk), pl.ds(half * both, both))
            total = dot(block, wgu[pieces[slot][half]])
            if slot == 0:
                acc[where] = total
            else:
                acc[where] += total

    def activate(chunk):
        first = acc[rows_of(chunk), pl.ds(0, both)]
        second = acc[rows_of(chunk), pl.ds(both, both)]
        total = first + pltpu.roll(second, chunk_rows - MOST_R, 0)
        inner = silu(total[:, :hidden_units]) * total[:, hidden_units:]
        _, half_of, _ = slot_parts((chunk_rows, hidden_units), 0)
        hid2[rows_of(chunk), pl.ds(0, hidden_units)] = jnp.where(
            half_of == 0, inner, 0.0
        ).astype(BF16)
        hid2[rows_of(chunk), pl.ds(hidden_units, hidden_units)] = jnp.where(
            half_of == 1, pltpu.roll(inner, MOST_R, 0), 0.0
        ).astype(BF16)

    partial = (outgoing.at[0], outgoing.at[1], for_left)

    def down(slot, owner, k):
        chunk = from_chunk(k)
        part = dot(hid2[rows_of(chunk), :], wed[owner])
        if slot is not None:
            partial[slot][pl.ds(chunk * per_chunk, per_chunk)] = part.reshape(
                per_chunk, 2 * MOST_R, wide
            ).astype(BF16)
        else:
            acc[rows_of(chunk), pl.ds(0, wide)] = part

    def e_copy(at, slot, k, landing, device):
        where = pl.ds(from_chunk(k) * per_chunk, per_chunk)
        return to(
            partial[slot].at[where],
            landing.at[where],
            e_send.at[at],
            e_recv.at[at],
            (dp, device),
        )

    relays, directs, passed = [], [], []
    for k in range(chunks):
        ahead, behind = ((1, right, e_left), (2, left, e_right))[:: 1 if k % 2 == 0 else -1]
        relays.append(e_copy(k, 0, k, e_relay, ahead[1]))
        directs.append(e_copy(4 + k, behind[0], k, behind[2], behind[1]))
        passed.append((ahead, e_copy(8 + k, ahead[0], k, ahead[2], ahead[1])))

    def pass_on(k):
        (slot, _, _), copy = passed[k]
        where = pl.ds(from_chunk(k) * per_chunk, per_chunk)
        relays[k].wait_recv()
        partial[slot][where] = (
            partial[slot][where].astype(F32) + e_relay[where].astype(F32)
        ).astype(BF16)
        copy.start()

    def finish(k):
        chunk = from_chunk(k)
        directs[k].wait_recv()
        passed[k][1].wait_recv()
        total = (
            acc[rows_of(chunk), pl.ds(0, wide)]
            + load_chunk(e_left, chunk)
            + load_chunk(e_right, chunk)
        )
        outgoing[2, pl.ds(chunk * per_chunk, per_chunk)] = total.reshape(
            per_chunk, 2 * MOST_R, wide
        ).astype(BF16)
        send_chunk(outgoing.at[2], came, chunk, c_send.at[0], c_recv.at[k], c_loc.at[0])

    first, second = range(chunks // 2), range(chunks // 2, chunks)
    for at in (0, 1):
        gathers[at].wait_recv()
        gathers[at + 2].start()
        gathers[at + 4].start()
    select(1)
    issue_next(*((1, k) for k in first))
    arrived_weights(wgu, 2)
    for k in range(chunks):
        expert_chunk(0, k)
    issue_next(*((1, k) for k in second))
    shared_step(1)
    for k in first:
        expert_chunk(1, k)
    for at in (2, 3):
        gathers[at].wait_recv()
    select(2)
    for at in (4, 5):
        gathers[at].wait_recv()
    select(3)
    issue_next((2, 0), (3, 0))
    shared_step(2)
    shared_step(3)

    shared_hidden = (
        silu(shared_acc[:, pl.ds(0, hidden_units)])
        * shared_acc[:, pl.ds(hidden_units, hidden_units)]
    ).astype(BF16)
    s_hidden[0] = shared_hidden
    hidden_sends = [
        to(
            s_hidden.at[0],
            s_hidden.at[place],
            s_send.at[3 + at],
            s_recv.at[3 + at],
            (dp, device),
        )
        for at, (device, place) in enumerate(((right, 3), (left, 1), (across, 2)))
    ]
    for copy in hidden_sends:
        copy.start()

    for k in second:
        expert_chunk(1, k)
    arrived_weights(wed, 4)

    def last_steps(k):
        expert_chunk(2, k)
        expert_chunk(3, k)
        activate(from_chunk(k))
        down(0, across, k)
        relays[k].start()
        slot, device = ((2, left), (1, right))[k % 2]
        down(slot, device, k)
        if k < chunks - 1:
            directs[k].start()
        (slot, device, _), _ = passed[k]
        down(slot, device, k)
        down(None, tp, k)

    for k in range(chunks):
        if k + 1 < chunks:
            issue_next((2, k + 1), (3, k + 1))
        last_steps(k)
        if k >= 1:
            pass_on(k - 1)
    wait_queue(len(queue))

    for copy in fetches:
        copy.wait_recv()

    @pl.loop(1, chips)
    def _(step):
        target = 2 * lax.rem(chip + step, chips) + core
        to(
            others.at[core, chip],
            others.at[core, chip],
            p_sem.at[0],
            p_sem.at[1],
            (target, tp),
        ).start()

    for k in range(chunks - 2):
        finish(k)
    passed[chunks - 2][1].wait_send()
    directs[chunks - 1].start()
    pass_on(chunks - 1)
    finish(chunks - 2)
    wait_peers(others.at[core], p_sem.at[1], chips - 1)
    swap = to(
        others.at[core], others.at[core], p_sem.at[2], p_sem.at[3], (dp + 1 - 2 * core, tp)
    )
    swap.start()
    finish(chunks - 1)

    for copy in hidden_sends:
        copy.wait_recv()
    arrived_weights(wsd, 3)
    swap.wait_recv()
    for half in range(2):
        total = dot(s_hidden[0], wsd[half])
        for place in range(TP - 1):
            total += dot(
                s_hidden[place + 1], others[half, :, place].reshape(hidden_units, wide)
            )
        s_own[pl.ds(half * rows, rows)] = total

    for k in range(chunks):
        wait_chunk(came, k, c_recv, c_loc.at[0])
        chunk = chunk_at(k)
        block = load_chunk(came, chunk).astype(BF16)
        s_own[...] += dot(back_hi[chunk], block) + dot(back_lo[chunk], block)
    keep = lax.broadcasted_iota(jnp.int32, (rows, wide), 0) < length
    for half in range(2):
        out_ref[:, pl.ds(half * wide, wide)] = jnp.where(
            keep, s_own[pl.ds(half * rows, rows)], 0.0
        ).astype(out_ref.dtype)

    sends = gathers + fetches + hidden_sends + [swap]
    for copy in sends + relays + directs + [copy for k, (_, copy) in enumerate(passed) if k != chunks - 2]:
        copy.wait_send()
    wait_peers(others.at[core], p_sem.at[0], chips - 1)
    wait_peers(outgoing.at[2], c_send.at[0], groups - 1)


def local(
    hidden_in,
    lengths,
    routes,
    route_weights,
    placement,
    shared_gate,
    shared_up,
    shared_down,
    expert_gate,
    expert_up,
    expert_down,
):
    groups = lax.axis_size("dp")
    rows, quarter = hidden_in.shape
    wide = quarter // 2
    pieces = 2 * TP
    units = shared_gate.shape[1]
    window = placement.shape[0]
    chunks = side_of(groups)
    packed = groups * 2 * MOST_R
    across_peers = (groups, 2 * MOST_R, wide)
    vmem = pl.BlockSpec(memory_space=pltpu.VMEM)
    smem = pl.BlockSpec(memory_space=pltpu.SMEM)
    hbm = pl.BlockSpec(memory_space=pl.ANY)
    dma = pltpu.SemaphoreType.DMA
    return pl.pallas_call(
        functools.partial(kernel, groups),
        out_shape=jax.ShapeDtypeStruct((rows, quarter), BF16),
        in_specs=[vmem] * 3 + [smem] + [hbm] * 7,
        out_specs=vmem,
        scratch_shapes=[
            pltpu.VMEM((pieces, wide, 2 * units), BF16),
            pltpu.VMEM((2, units, wide), BF16),
            pltpu.VMEM((pieces, wide, 2 * units), BF16),
            pltpu.VMEM((TP, 2 * units, wide), BF16),
            pltpu.VMEM((TP, 2 * rows, wide), BF16),
            pltpu.VMEM((packed, 2 * rows), BF16),
            pltpu.VMEM((chunks, 2 * rows, packed // chunks), BF16),
            pltpu.VMEM((chunks, 2 * rows, packed // chunks), BF16),
            pltpu.VMEM((TP,) + across_peers, BF16),
            pltpu.VMEM((TP,) + across_peers, BF16),
            pltpu.VMEM((packed, 4 * units), F32),
            pltpu.VMEM((rows, 2 * units), F32),
            pltpu.VMEM((packed, 2 * units), BF16),
            pltpu.VMEM((TP, rows, units), BF16),
            pltpu.VMEM((2 * rows, wide), F32),
            pltpu.VMEM((2, groups // 2, TP - 1, 2 * units // groups, wide), BF16),
            pltpu.VMEM(across_peers, BF16),
            pltpu.VMEM(across_peers, BF16),
            pltpu.VMEM(across_peers, BF16),
            pltpu.VMEM(across_peers, BF16),
            pltpu.VMEM(across_peers, BF16),
            dma((5,)),
            dma((6,)),
            dma((6,)),
            dma((TP, chunks)),
            dma((TP, chunks)),
            dma((TP,)),
            dma((6,)),
            dma((6,)),
            dma((4,)),
            dma((12,)),
            dma((12,)),
            dma((1,)),
            dma((chunks,)),
            dma((1,)),
        ],
        compiler_params=pltpu.CompilerParams(
            collective_id=0, has_side_effects=True, vmem_limit_bytes=62 << 20
        ),
        cost_estimate=pl.CostEstimate(
            flops=2 * 5 * rows * quarter * 4 * units * 3 // 2,
            bytes_accessed=6 * quarter * 4 * units * 2,
            transcendentals=0,
        ),
    )(
        routes.T,
        route_weights.T,
        placement.reshape(1, window),
        lengths,
        hidden_in,
        shared_gate.reshape(pieces, wide, units),
        shared_up.reshape(pieces, wide, units),
        shared_down,
        expert_gate.reshape(pieces, wide, units),
        expert_up.reshape(pieces, wide, units),
        expert_down[0],
    )


def solution(mesh):
    in_specs = (
        P("dp", "tp"),
        P("dp"),
        P("dp", None),
        P("dp", None),
        P(),
        P(None, "tp"),
        P(None, "tp"),
        P("tp", None),
        P("dp", None, "tp"),
        P("dp", None, "tp"),
        P("dp", "tp", None),
    )
    out_specs = P("dp", "tp")
    return jax.shard_map(local, mesh=mesh, in_specs=in_specs, out_specs=out_specs, check_vma=False)
```

```python
import functools
import math

import jax
import jax.numpy as jnp
from jax import lax
from jax.experimental import pallas as pl
from jax.experimental.pallas import tpu as pltpu
from jax.sharding import PartitionSpec as P

MOST_R = 12
MESH = pl.DeviceIdType.MESH
BF16 = jnp.bfloat16
F32 = jnp.float32
TP = 4
WINDOW = 4


def dot(a, b):
    return jnp.dot(a, b, preferred_element_type=F32)


def silu(v):
    return v / (1.0 + jnp.exp(-v))


def slot_parts(shape, axis):
    at = lax.broadcasted_iota(jnp.int32, shape, axis)
    group = (at * 2731) >> 16
    place = at - group * (2 * MOST_R)
    half = (place >= MOST_R).astype(jnp.int32)
    return group, half, place - MOST_R * half


def side_of(groups):
    side = math.isqrt(groups // 2)
    assert 2 * side * side == groups and side & (side - 1) == 0
    return side


def device_at(place, side):
    bits = side.bit_length() - 1
    chunk = place >> (bits + 1)
    x = (place >> 1) & (side - 1)
    z = (chunk + side - x) & (side - 1)
    return 2 * (side * x + z) + (place & 1)


def kernel(
    groups,
    routes_ref,
    weights_ref,
    placement_ref,
    length_ref,
    hidden_ref,
    sg_ref,
    su_ref,
    sd_ref,
    eg_ref,
    eu_ref,
    ed_ref,
    out_ref,
    wsgu,
    wsd,
    wgu,
    wed,
    held,
    sel,
    back_hi,
    back_lo,
    outgoing,
    arrived,
    acc,
    shared_acc,
    hid2,
    s_hidden,
    s_own,
    others,
    for_left,
    e_relay,
    e_left,
    e_right,
    came,
    w_sem,
    ag_send,
    ag_recv,
    d_send,
    d_recv,
    d_loc,
    s_send,
    s_recv,
    p_sem,
    e_send,
    e_recv,
    c_send,
    c_recv,
    c_loc,
):
    dp = lax.axis_index("dp")
    tp = lax.axis_index("tp")
    right = lax.rem(tp + 1, TP)
    left = lax.rem(tp + TP - 1, TP)
    across = lax.rem(tp + 2, TP)
    rows = held.shape[1] // 2
    wide = held.shape[2]
    window = placement_ref.shape[1]
    chunks = side_of(groups)
    hidden_units = ed_ref.shape[0]
    per_chunk = groups // chunks
    chunk_rows = per_chunk * 2 * MOST_R
    packed = groups * 2 * MOST_R
    top = routes_ref.shape[0]
    pieces = (
        (2 * tp, 2 * tp + 1),
        (2 * left, 2 * right + 1),
        (2 * left + 1, 2 * right),
        (2 * across, 2 * across + 1),
    )

    for half in range(2):
        pltpu.make_async_copy(
            hidden_ref.at[:, pl.ds(half * wide, wide)],
            held.at[0, pl.ds(half * rows, rows)],
            w_sem.at[0],
        ).start()
    for at, (gate, up, both) in enumerate(((sg_ref, su_ref, wsgu), (eg_ref, eu_ref, wgu))):
        for part, source in enumerate((gate, up)):
            pltpu.make_async_copy(
                source,
                both.at[:, :, pl.ds(part * hidden_units, hidden_units)],
                w_sem.at[1 + at],
            ).start()
    def columns(piece):
        return pl.ds(pl.multiple_of(piece * wide, wide), wide)

    for half in range(2):
        pltpu.make_async_copy(
            sd_ref.at[:, columns(2 * tp + half)], wsd.at[half], w_sem.at[3]
        ).start()
    for piece in range(2 * TP):
        pltpu.make_async_copy(
            ed_ref.at[:, pl.ds(piece * wide, wide)],
            wed.at[piece // 2, pl.ds((piece % 2) * hidden_units, hidden_units)],
            w_sem.at[4],
        ).start()

    def arrived_weights(ref, at):
        pltpu.make_async_copy(ref, ref, w_sem.at[at]).wait()

    barrier = pltpu.get_barrier_semaphore()

    @pl.loop(1, groups)
    def _(step):
        pl.semaphore_signal(
            barrier,
            inc=1,
            device_id=(lax.rem(dp + step, groups), tp),
            device_id_type=MESH,
        )

    for neighbour in (left, right, across):
        pl.semaphore_signal(barrier, inc=1, device_id=(dp, neighbour), device_id_type=MESH)

    length = length_ref[0]
    live = lax.broadcasted_iota(jnp.int32, (window, rows), 1) < length
    expert_at = lax.broadcasted_iota(jnp.int32, (window, rows), 0)
    named = jnp.zeros((window, rows), F32)
    scale = jnp.zeros((window, rows), F32)
    for k in range(top):
        match = routes_ref[pl.ds(k, 1), :] == expert_at
        named = named + jnp.where(match, 1.0, 0.0)
        scale = scale + jnp.where(match, weights_ref[pl.ds(k, 1), :], 0.0)
    named = jnp.where(live, named, 0.0)
    before = jnp.where(
        lax.broadcasted_iota(jnp.int32, (rows, rows), 0)
        < lax.broadcasted_iota(jnp.int32, (rows, rows), 1),
        1.0,
        0.0,
    ).astype(BF16)
    place = jnp.where(named > 0.0, dot(named.astype(BF16), before), -1.0)
    group_of, _, _ = slot_parts((packed, window), 0)
    spread = jnp.where(placement_ref[...] == device_at(group_of, chunks), 1.0, 0.0).astype(BF16)
    _, half_of, want = slot_parts((packed, rows), 0)
    hit = dot(spread, place.astype(BF16)) == want.astype(F32)
    for half in range(2):
        sel[:, pl.ds(half * rows, rows)] = jnp.where(
            hit, jnp.where(half_of == half, 1.0, 0.0), 0.0
        ).astype(BF16)

    pl.semaphore_wait(barrier, groups - 1 + 3)

    def to(src, dst, send, recv, device):
        return pltpu.make_async_remote_copy(
            src_ref=src,
            dst_ref=dst,
            send_sem=send,
            recv_sem=recv,
            device_id=device,
            device_id_type=MESH,
        )

    arrived_weights(held.at[0], 0)

    def half_block(slot, half):
        return held.at[slot, pl.ds(half * rows, rows)]

    gathers = []
    for at, (source, half, target, landing, device) in enumerate(
        (
            (0, 0, 1, 0, right),
            (0, 1, 1, 1, left),
            (0, 1, 2, 0, right),
            (0, 0, 2, 1, left),
            (1, 0, 3, 0, right),
            (1, 1, 3, 1, left),
        )
    ):
        gathers.append(
            to(
                half_block(source, half),
                half_block(target, landing),
                ag_send.at[at],
                ag_recv.at[at],
                (dp, device),
            )
        )
    for at in range(2):
        gathers[at].start()

    chips = groups // 2
    core = lax.rem(dp, 2)
    chip_x, chip_z = dp // (2 * chunks), lax.rem(dp // 2, chunks)
    near = core * chip_x + (1 - core) * chip_z
    far = core * chip_z + (1 - core) * chip_x
    mine = far * chunks + near

    def spread_to(near_at, far_at):
        x = core * near_at + (1 - core) * far_at
        z = core * far_at + (1 - core) * near_at
        return (2 * (x * chunks + z) + core, tp)

    share = others.shape[3]

    fetches = [
        to(
            sd_ref.at[pl.ds(pl.multiple_of(mine * share, share), share), columns(2 * device + core)],
            others.at[core, mine, place],
            s_send.at[at],
            s_recv.at[at],
            (dp, device),
        )
        for at, (device, place) in enumerate(((right, 2), (left, 0), (across, 1)))
    ]
    for copy in fetches:
        copy.start()

    my_x = dp // per_chunk
    my_chunk = lax.rem(my_x + lax.rem(dp // 2, chunks), chunks)
    my_place_in = 2 * my_x + lax.rem(dp, 2)
    me = my_chunk * per_chunk + my_place_in

    def rows_of(chunk):
        return pl.ds(pl.multiple_of(chunk * chunk_rows, chunk_rows), chunk_rows)

    def chunk_at(k):
        return lax.rem(my_chunk + k, chunks)

    def send_chunk(source, landing, chunk, send, recv, local):
        @pl.loop(0, per_chunk)
        def _(step):
            place = lax.rem(my_place_in + step, per_chunk)
            x = place // 2
            device = 2 * (chunks * x + lax.rem(chunk + chunks - x, chunks)) + lax.rem(place, 2)
            there = chunk * per_chunk + place

            @pl.when(device != dp)
            def _():
                to(source.at[there], landing.at[me], send, recv, (device, tp)).start()

            @pl.when(device == dp)
            def _():
                pltpu.make_async_copy(source.at[me], landing.at[me], local).start()

    def wait_peers(ref, sem, number):
        view = ref.at[pl.ds(0, number)]
        pltpu.make_async_copy(view, view, sem).wait()

    def from_chunk(k):
        return lax.rem(my_chunk + chunks - k, chunks)

    def wait_chunk(ref, k, recv, local):
        wait_peers(ref, recv.at[k], per_chunk - 1 if k == 0 else per_chunk)
        if k == 0:
            wait_peers(ref, local, 1)

    def issue(slot, k):
        send_chunk(
            outgoing.at[slot],
            arrived.at[slot],
            chunk_at(k),
            d_send.at[slot, k],
            d_recv.at[slot, k],
            d_loc.at[slot],
        )

    def wait_issued(slot, k):
        wait_peers(outgoing.at[slot], d_send.at[slot, k], per_chunk - (k == 0))

    queue = [(0, k) for k in range(chunks)]
    waited = []

    def wait_queue(number):
        while len(waited) < number:
            wait_issued(*queue[len(waited)])
            waited.append(1)

    def issue_next(*which):
        for slot, k in which:
            wait_queue(len(queue) + 1 - WINDOW)
            issue(slot, k)
            queue.append((slot, k))

    def select(slot):
        @pl.loop(0, chunks)
        def _(k):
            chunk = chunk_at(k)
            picked = dot(sel[rows_of(chunk), :], held[slot])
            outgoing[slot, pl.ds(chunk * per_chunk, per_chunk)] = picked.reshape(
                per_chunk, 2 * MOST_R, wide
            ).astype(BF16)
            if slot == 0:
                issue(slot, k)

    def shared_step(slot):
        first, second = pieces[slot]
        total = dot(held[slot, pl.ds(0, rows)], wsgu[first]) + dot(
            held[slot, pl.ds(rows, rows)], wsgu[second]
        )
        if slot == 0:
            shared_acc[...] = total
        else:
            shared_acc[...] += total

    def load_chunk(ref, k):
        return ref[pl.ds(k * per_chunk, per_chunk)].astype(F32).reshape(chunk_rows, wide)

    select(0)
    arrived_weights(wsgu, 1)
    shared_step(0)

    place = jnp.transpose(place).astype(BF16)
    scale = jnp.transpose(scale)
    head = scale.astype(BF16)
    rest = (scale - head.astype(F32)).astype(BF16)
    placement_col = jnp.transpose(
        jnp.broadcast_to(placement_ref[...].astype(F32), (8, window))
    )[:, :1]
    for chunk in range(chunks):
        group_of, _, _ = slot_parts((window, chunk_rows), 1)
        group_of = device_at(group_of + chunk * per_chunk, chunks).astype(F32)
        spread = jnp.where(placement_col == group_of, 1.0, 0.0).astype(BF16)
        _, half_of, want = slot_parts((rows, chunk_rows), 1)
        hit = dot(place, spread) == want.astype(F32)
        for part, kept in ((head, back_hi), (rest, back_lo)):
            value = jnp.where(hit, dot(part, spread), 0.0)
            for half in range(2):
                kept[chunk, pl.ds(half * rows, rows), :] = jnp.where(
                    half_of == half, value, 0.0
                ).astype(BF16)

    both = 2 * hidden_units

    def expert_chunk(slot, k):
        wait_chunk(arrived.at[slot], k, d_recv.at[slot], d_loc.at[slot])
        chunk = from_chunk(k)
        block = load_chunk(arrived.at[slot], chunk).astype(BF16)
        for half in range(2):
            where = (rows_of(chunk), pl.ds(half * both, both))
            total = dot(block, wgu[pieces[slot][half]])
            if slot == 0:
                acc[where] = total
            else:
                acc[where] += total

    def activate(chunk):
        first = acc[rows_of(chunk), pl.ds(0, both)]
        second = acc[rows_of(chunk), pl.ds(both, both)]
        total = first + pltpu.roll(second, chunk_rows - MOST_R, 0)
        inner = silu(total[:, :hidden_units]) * total[:, hidden_units:]
        _, half_of, _ = slot_parts((chunk_rows, hidden_units), 0)
        hid2[rows_of(chunk), pl.ds(0, hidden_units)] = jnp.where(
            half_of == 0, inner, 0.0
        ).astype(BF16)
        hid2[rows_of(chunk), pl.ds(hidden_units, hidden_units)] = jnp.where(
            half_of == 1, pltpu.roll(inner, MOST_R, 0), 0.0
        ).astype(BF16)

    partial = (outgoing.at[0], outgoing.at[1], for_left)

    def down(slot, owner, k):
        chunk = from_chunk(k)
        part = dot(hid2[rows_of(chunk), :], wed[owner])
        if slot is not None:
            partial[slot][pl.ds(chunk * per_chunk, per_chunk)] = part.reshape(
                per_chunk, 2 * MOST_R, wide
            ).astype(BF16)
        else:
            acc[rows_of(chunk), pl.ds(0, wide)] = part

    def e_copy(at, slot, k, landing, device):
        where = pl.ds(from_chunk(k) * per_chunk, per_chunk)
        return to(
            partial[slot].at[where],
            landing.at[where],
            e_send.at[at],
            e_recv.at[at],
            (dp, device),
        )

    relays, directs, passed = [], [], []
    for k in range(chunks):
        ahead, behind = ((1, right, e_left), (2, left, e_right))[:: 1 if k % 2 == 0 else -1]
        relays.append(e_copy(k, 0, k, e_relay, ahead[1]))
        directs.append(e_copy(4 + k, behind[0], k, behind[2], behind[1]))
        passed.append((ahead, e_copy(8 + k, ahead[0], k, ahead[2], ahead[1])))

    def pass_on(k):
        (slot, _, _), copy = passed[k]
        where = pl.ds(from_chunk(k) * per_chunk, per_chunk)
        relays[k].wait_recv()
        partial[slot][where] = (
            partial[slot][where].astype(F32) + e_relay[where].astype(F32)
        ).astype(BF16)
        copy.start()

    def finish(k):
        chunk = from_chunk(k)
        directs[k].wait_recv()
        passed[k][1].wait_recv()
        total = (
            acc[rows_of(chunk), pl.ds(0, wide)]
            + load_chunk(e_left, chunk)
            + load_chunk(e_right, chunk)
        )
        outgoing[2, pl.ds(chunk * per_chunk, per_chunk)] = total.reshape(
            per_chunk, 2 * MOST_R, wide
        ).astype(BF16)
        send_chunk(outgoing.at[2], came, chunk, c_send.at[0], c_recv.at[k], c_loc.at[0])

    first, second = range(chunks // 2), range(chunks // 2, chunks)
    for at in (0, 1):
        gathers[at].wait_recv()
        gathers[at + 2].start()
        gathers[at + 4].start()
    select(1)
    issue_next(*((1, k) for k in first))
    arrived_weights(wgu, 2)
    for k in range(chunks):
        expert_chunk(0, k)
    issue_next(*((1, k) for k in second))
    shared_step(1)
    for k in first:
        expert_chunk(1, k)
    for at in (2, 3):
        gathers[at].wait_recv()
    select(2)
    for copy in fetches:
        copy.wait_recv()

    @pl.loop(1, chunks)
    def _(step):
        piece = others.at[core, mine]
        device = spread_to(lax.rem(near + step, chunks), far)
        to(piece, piece, p_sem.at[0], p_sem.at[1], device).start()

    for at in (4, 5):
        gathers[at].wait_recv()
    select(3)
    issue_next((2, 0), (3, 0))
    shared_step(2)
    shared_step(3)

    shared_hidden = (
        silu(shared_acc[:, pl.ds(0, hidden_units)])
        * shared_acc[:, pl.ds(hidden_units, hidden_units)]
    ).astype(BF16)
    s_hidden[0] = shared_hidden
    hidden_sends = [
        to(
            s_hidden.at[0],
            s_hidden.at[place],
            s_send.at[3 + at],
            s_recv.at[3 + at],
            (dp, device),
        )
        for at, (device, place) in enumerate(((right, 3), (left, 1), (across, 2)))
    ]
    for copy in hidden_sends:
        copy.start()

    for k in second:
        expert_chunk(1, k)
    arrived_weights(wed, 4)

    def last_steps(k):
        expert_chunk(2, k)
        expert_chunk(3, k)
        activate(from_chunk(k))
        down(0, across, k)
        relays[k].start()
        slot, device = ((2, left), (1, right))[k % 2]
        down(slot, device, k)
        if k < chunks - 1:
            directs[k].start()
        (slot, device, _), _ = passed[k]
        down(slot, device, k)
        down(None, tp, k)

    for k in range(chunks):
        if k + 1 < chunks:
            issue_next((2, k + 1), (3, k + 1))
        last_steps(k)
        if k >= 1:
            pass_on(k - 1)
    wait_queue(len(queue))

    wait_peers(others.at[core], p_sem.at[1], chunks - 1)

    @pl.loop(1, chunks)
    def _(step):
        line = others.at[core, pl.ds(far * chunks, chunks)]
        device = spread_to(near, lax.rem(far + step, chunks))
        to(line, line, p_sem.at[4], p_sem.at[5], device).start()

    for k in range(chunks - 2):
        finish(k)
    passed[chunks - 2][1].wait_send()
    directs[chunks - 1].start()
    pass_on(chunks - 1)
    finish(chunks - 2)
    wait_peers(others.at[core], p_sem.at[5], chips - chunks)
    swap = to(
        others.at[core], others.at[core], p_sem.at[2], p_sem.at[3], (dp + 1 - 2 * core, tp)
    )
    swap.start()
    finish(chunks - 1)

    for copy in hidden_sends:
        copy.wait_recv()
    arrived_weights(wsd, 3)
    swap.wait_recv()
    for half in range(2):
        total = dot(s_hidden[0], wsd[half])
        for place in range(TP - 1):
            total += dot(
                s_hidden[place + 1], others[half, :, place].reshape(hidden_units, wide)
            )
        s_own[pl.ds(half * rows, rows)] = total

    for k in range(chunks):
        wait_chunk(came, k, c_recv, c_loc.at[0])
        chunk = chunk_at(k)
        block = load_chunk(came, chunk).astype(BF16)
        s_own[...] += dot(back_hi[chunk], block) + dot(back_lo[chunk], block)
    keep = lax.broadcasted_iota(jnp.int32, (rows, wide), 0) < length
    for half in range(2):
        out_ref[:, pl.ds(half * wide, wide)] = jnp.where(
            keep, s_own[pl.ds(half * rows, rows)], 0.0
        ).astype(out_ref.dtype)

    sends = gathers + fetches + hidden_sends + [swap]
    for copy in sends + relays + directs + [copy for k, (_, copy) in enumerate(passed) if k != chunks - 2]:
        copy.wait_send()
    wait_peers(others.at[core], p_sem.at[0], chunks - 1)
    wait_peers(others.at[core], p_sem.at[4], chips - chunks)
    wait_peers(outgoing.at[2], c_send.at[0], groups - 1)


def local(
    hidden_in,
    lengths,
    routes,
    route_weights,
    placement,
    shared_gate,
    shared_up,
    shared_down,
    expert_gate,
    expert_up,
    expert_down,
):
    groups = lax.axis_size("dp")
    rows, quarter = hidden_in.shape
    wide = quarter // 2
    pieces = 2 * TP
    units = shared_gate.shape[1]
    window = placement.shape[0]
    chunks = side_of(groups)
    packed = groups * 2 * MOST_R
    across_peers = (groups, 2 * MOST_R, wide)
    vmem = pl.BlockSpec(memory_space=pltpu.VMEM)
    smem = pl.BlockSpec(memory_space=pltpu.SMEM)
    hbm = pl.BlockSpec(memory_space=pl.ANY)
    dma = pltpu.SemaphoreType.DMA
    return pl.pallas_call(
        functools.partial(kernel, groups),
        out_shape=jax.ShapeDtypeStruct((rows, quarter), BF16),
        in_specs=[vmem] * 3 + [smem] + [hbm] * 7,
        out_specs=vmem,
        scratch_shapes=[
            pltpu.VMEM((pieces, wide, 2 * units), BF16),
            pltpu.VMEM((2, units, wide), BF16),
            pltpu.VMEM((pieces, wide, 2 * units), BF16),
            pltpu.VMEM((TP, 2 * units, wide), BF16),
            pltpu.VMEM((TP, 2 * rows, wide), BF16),
            pltpu.VMEM((packed, 2 * rows), BF16),
            pltpu.VMEM((chunks, 2 * rows, packed // chunks), BF16),
            pltpu.VMEM((chunks, 2 * rows, packed // chunks), BF16),
            pltpu.VMEM((TP,) + across_peers, BF16),
            pltpu.VMEM((TP,) + across_peers, BF16),
            pltpu.VMEM((packed, 4 * units), F32),
            pltpu.VMEM((rows, 2 * units), F32),
            pltpu.VMEM((packed, 2 * units), BF16),
            pltpu.VMEM((TP, rows, units), BF16),
            pltpu.VMEM((2 * rows, wide), F32),
            pltpu.VMEM((2, groups // 2, TP - 1, 2 * units // groups, wide), BF16),
            pltpu.VMEM(across_peers, BF16),
            pltpu.VMEM(across_peers, BF16),
            pltpu.VMEM(across_peers, BF16),
            pltpu.VMEM(across_peers, BF16),
            pltpu.VMEM(across_peers, BF16),
            dma((5,)),
            dma((6,)),
            dma((6,)),
            dma((TP, chunks)),
            dma((TP, chunks)),
            dma((TP,)),
            dma((6,)),
            dma((6,)),
            dma((6,)),
            dma((12,)),
            dma((12,)),
            dma((1,)),
            dma((chunks,)),
            dma((1,)),
        ],
        compiler_params=pltpu.CompilerParams(
            collective_id=0, has_side_effects=True, vmem_limit_bytes=62 << 20
        ),
        cost_estimate=pl.CostEstimate(
            flops=2 * 5 * rows * quarter * 4 * units * 3 // 2,
            bytes_accessed=6 * quarter * 4 * units * 2,
            transcendentals=0,
        ),
    )(
        routes.T,
        route_weights.T,
        placement.reshape(1, window),
        lengths,
        hidden_in,
        shared_gate.reshape(pieces, wide, units),
        shared_up.reshape(pieces, wide, units),
        shared_down,
        expert_gate.reshape(pieces, wide, units),
        expert_up.reshape(pieces, wide, units),
        expert_down[0],
    )


def solution(mesh):
    in_specs = (
        P("dp", "tp"),
        P("dp"),
        P("dp", None),
        P("dp", None),
        P(),
        P(None, "tp"),
        P(None, "tp"),
        P("tp", None),
        P("dp", None, "tp"),
        P("dp", None, "tp"),
        P("dp", "tp", None),
    )
    out_specs = P("dp", "tp")
    return jax.shard_map(local, mesh=mesh, in_specs=in_specs, out_specs=out_specs, check_vma=False)
```

```python
import functools
import math

import jax
import jax.numpy as jnp
from jax import lax
from jax.experimental import pallas as pl
from jax.experimental.pallas import tpu as pltpu
from jax.sharding import PartitionSpec as P

MOST_R = 12
MESH = pl.DeviceIdType.MESH
BF16 = jnp.bfloat16
F32 = jnp.float32
TP = 4
WINDOW = 4


def dot(a, b):
    return jnp.dot(a, b, preferred_element_type=F32)


def silu(v):
    return v / (1.0 + jnp.exp(-v))


def slot_parts(shape, axis):
    at = lax.broadcasted_iota(jnp.int32, shape, axis)
    group = (at * 2731) >> 16
    place = at - group * (2 * MOST_R)
    half = (place >= MOST_R).astype(jnp.int32)
    return group, half, place - MOST_R * half


def side_of(groups):
    side = math.isqrt(groups // 2)
    assert 2 * side * side == groups and side & (side - 1) == 0
    return side


def device_at(place, side):
    bits = side.bit_length() - 1
    chunk = place >> (bits + 1)
    x = (place >> 1) & (side - 1)
    z = (chunk + side - x) & (side - 1)
    return 2 * (side * x + z) + (place & 1)


def kernel(
    groups,
    routes_ref,
    weights_ref,
    placement_ref,
    length_ref,
    hidden_ref,
    sg_ref,
    su_ref,
    sd_ref,
    eg_ref,
    eu_ref,
    ed_ref,
    out_ref,
    wsgu,
    wsd,
    wgu,
    wed,
    held,
    sel,
    back_hi,
    back_lo,
    outgoing,
    arrived,
    acc,
    shared_acc,
    hid2,
    s_hidden,
    s_own,
    others,
    for_left,
    e_relay,
    e_left,
    e_right,
    came,
    w_sem,
    ag_send,
    ag_recv,
    d_send,
    d_recv,
    d_loc,
    s_send,
    s_recv,
    p_sem,
    e_send,
    e_recv,
    c_send,
    c_recv,
    c_loc,
):
    dp = lax.axis_index("dp")
    tp = lax.axis_index("tp")
    right = lax.rem(tp + 1, TP)
    left = lax.rem(tp + TP - 1, TP)
    across = lax.rem(tp + 2, TP)
    rows = held.shape[1] // 2
    wide = held.shape[2]
    window = placement_ref.shape[1]
    chunks = side_of(groups)
    hidden_units = ed_ref.shape[0]
    per_chunk = groups // chunks
    chunk_rows = per_chunk * 2 * MOST_R
    packed = groups * 2 * MOST_R
    top = routes_ref.shape[0]
    pieces = (
        (2 * tp, 2 * tp + 1),
        (2 * left, 2 * right + 1),
        (2 * left + 1, 2 * right),
        (2 * across, 2 * across + 1),
    )

    for half in range(2):
        pltpu.make_async_copy(
            hidden_ref.at[:, pl.ds(half * wide, wide)],
            held.at[0, pl.ds(half * rows, rows)],
            w_sem.at[0],
        ).start()
    for at, (gate, up, both) in enumerate(((sg_ref, su_ref, wsgu), (eg_ref, eu_ref, wgu))):
        for part, source in enumerate((gate, up)):
            pltpu.make_async_copy(
                source,
                both.at[:, :, pl.ds(part * hidden_units, hidden_units)],
                w_sem.at[1 + at],
            ).start()
    def columns(piece):
        return pl.ds(pl.multiple_of(piece * wide, wide), wide)

    for half in range(2):
        pltpu.make_async_copy(
            sd_ref.at[:, columns(2 * tp + half)], wsd.at[half], w_sem.at[3]
        ).start()
    for piece in range(2 * TP):
        pltpu.make_async_copy(
            ed_ref.at[:, pl.ds(piece * wide, wide)],
            wed.at[piece // 2, pl.ds((piece % 2) * hidden_units, hidden_units)],
            w_sem.at[4],
        ).start()

    def arrived_weights(ref, at):
        pltpu.make_async_copy(ref, ref, w_sem.at[at]).wait()

    barrier = pltpu.get_barrier_semaphore()

    @pl.loop(1, groups)
    def _(step):
        pl.semaphore_signal(
            barrier,
            inc=1,
            device_id=(lax.rem(dp + step, groups), tp),
            device_id_type=MESH,
        )

    for neighbour in (left, right, across):
        pl.semaphore_signal(barrier, inc=1, device_id=(dp, neighbour), device_id_type=MESH)

    length = length_ref[0]
    live = lax.broadcasted_iota(jnp.int32, (window, rows), 1) < length
    expert_at = lax.broadcasted_iota(jnp.int32, (window, rows), 0)
    named = jnp.zeros((window, rows), F32)
    scale = jnp.zeros((window, rows), F32)
    for k in range(top):
        match = routes_ref[pl.ds(k, 1), :] == expert_at
        named = named + jnp.where(match, 1.0, 0.0)
        scale = scale + jnp.where(match, weights_ref[pl.ds(k, 1), :], 0.0)
    named = jnp.where(live, named, 0.0)
    before = jnp.where(
        lax.broadcasted_iota(jnp.int32, (rows, rows), 0)
        < lax.broadcasted_iota(jnp.int32, (rows, rows), 1),
        1.0,
        0.0,
    ).astype(BF16)
    place = jnp.where(named > 0.0, dot(named.astype(BF16), before), -1.0)
    group_of, _, _ = slot_parts((packed, window), 0)
    spread = jnp.where(placement_ref[...] == device_at(group_of, chunks), 1.0, 0.0).astype(BF16)
    _, half_of, want = slot_parts((packed, rows), 0)
    hit = dot(spread, place.astype(BF16)) == want.astype(F32)
    for half in range(2):
        sel[:, pl.ds(half * rows, rows)] = jnp.where(
            hit, jnp.where(half_of == half, 1.0, 0.0), 0.0
        ).astype(BF16)

    pl.semaphore_wait(barrier, groups - 1 + 3)

    def to(src, dst, send, recv, device):
        return pltpu.make_async_remote_copy(
            src_ref=src,
            dst_ref=dst,
            send_sem=send,
            recv_sem=recv,
            device_id=device,
            device_id_type=MESH,
        )

    arrived_weights(held.at[0], 0)

    def half_block(slot, half):
        return held.at[slot, pl.ds(half * rows, rows)]

    gathers = []
    for at, (source, half, target, landing, device) in enumerate(
        (
            (0, 0, 1, 0, right),
            (0, 1, 1, 1, left),
            (0, 1, 2, 0, right),
            (0, 0, 2, 1, left),
            (1, 0, 3, 0, right),
            (1, 1, 3, 1, left),
        )
    ):
        gathers.append(
            to(
                half_block(source, half),
                half_block(target, landing),
                ag_send.at[at],
                ag_recv.at[at],
                (dp, device),
            )
        )
    for at in range(2):
        gathers[at].start()

    chips = groups // 2
    core = lax.rem(dp, 2)
    chip_x, chip_z = dp // (2 * chunks), lax.rem(dp // 2, chunks)
    near = core * chip_x + (1 - core) * chip_z
    far = core * chip_z + (1 - core) * chip_x
    mine = far * chunks + near

    def spread_to(near_at, far_at):
        x = core * near_at + (1 - core) * far_at
        z = core * far_at + (1 - core) * near_at
        return (2 * (x * chunks + z) + core, tp)

    share = others.shape[3]

    fetches = [
        to(
            sd_ref.at[pl.ds(pl.multiple_of(mine * share, share), share), columns(2 * device + core)],
            others.at[core, mine, place],
            s_send.at[at],
            s_recv.at[at],
            (dp, device),
        )
        for at, (device, place) in enumerate(((right, 2), (left, 0), (across, 1)))
    ]
    for copy in fetches:
        copy.start()

    my_x = dp // per_chunk
    my_chunk = lax.rem(my_x + lax.rem(dp // 2, chunks), chunks)
    my_place_in = 2 * my_x + lax.rem(dp, 2)
    me = my_chunk * per_chunk + my_place_in

    def rows_of(chunk):
        return pl.ds(pl.multiple_of(chunk * chunk_rows, chunk_rows), chunk_rows)

    def chunk_at(k):
        return lax.rem(my_chunk + k, chunks)

    def send_chunk(source, landing, chunk, send, recv, local):
        @pl.loop(0, per_chunk)
        def _(step):
            place = lax.rem(my_place_in + step, per_chunk)
            x = place // 2
            device = 2 * (chunks * x + lax.rem(chunk + chunks - x, chunks)) + lax.rem(place, 2)
            there = chunk * per_chunk + place

            @pl.when(device != dp)
            def _():
                to(source.at[there], landing.at[me], send, recv, (device, tp)).start()

            @pl.when(device == dp)
            def _():
                pltpu.make_async_copy(source.at[me], landing.at[me], local).start()

    def wait_peers(ref, sem, number):
        view = ref.at[pl.ds(0, number)]
        pltpu.make_async_copy(view, view, sem).wait()

    def from_chunk(k):
        return lax.rem(my_chunk + chunks - k, chunks)

    def wait_chunk(ref, k, recv, local):
        wait_peers(ref, recv.at[k], per_chunk - 1 if k == 0 else per_chunk)
        if k == 0:
            wait_peers(ref, local, 1)

    def issue(slot, k):
        send_chunk(
            outgoing.at[slot],
            arrived.at[slot],
            chunk_at(k),
            d_send.at[slot, k],
            d_recv.at[slot, k],
            d_loc.at[slot],
        )

    def wait_issued(slot, k):
        wait_peers(outgoing.at[slot], d_send.at[slot, k], per_chunk - (k == 0))

    queue = [(0, k) for k in range(chunks)]
    waited = []

    def wait_queue(number):
        while len(waited) < number:
            wait_issued(*queue[len(waited)])
            waited.append(1)

    def issue_next(*which):
        for slot, k in which:
            wait_queue(len(queue) + 1 - WINDOW)
            issue(slot, k)
            queue.append((slot, k))

    def select(slot):
        @pl.loop(0, chunks)
        def _(k):
            chunk = chunk_at(k)
            picked = dot(sel[rows_of(chunk), :], held[slot])
            outgoing[slot, pl.ds(chunk * per_chunk, per_chunk)] = picked.reshape(
                per_chunk, 2 * MOST_R, wide
            ).astype(BF16)
            if slot == 0:
                issue(slot, k)

    def shared_step(slot):
        first, second = pieces[slot]
        total = dot(held[slot, pl.ds(0, rows)], wsgu[first]) + dot(
            held[slot, pl.ds(rows, rows)], wsgu[second]
        )
        if slot == 0:
            shared_acc[...] = total
        else:
            shared_acc[...] += total

    def load_chunk(ref, k):
        return ref[pl.ds(k * per_chunk, per_chunk)].astype(F32).reshape(chunk_rows, wide)

    select(0)
    arrived_weights(wsgu, 1)
    shared_step(0)

    place = jnp.transpose(place).astype(BF16)
    scale = jnp.transpose(scale)
    head = scale.astype(BF16)
    rest = (scale - head.astype(F32)).astype(BF16)
    placement_col = jnp.transpose(
        jnp.broadcast_to(placement_ref[...].astype(F32), (8, window))
    )[:, :1]
    for chunk in range(chunks):
        group_of, _, _ = slot_parts((window, chunk_rows), 1)
        group_of = device_at(group_of + chunk * per_chunk, chunks).astype(F32)
        spread = jnp.where(placement_col == group_of, 1.0, 0.0).astype(BF16)
        _, half_of, want = slot_parts((rows, chunk_rows), 1)
        hit = dot(place, spread) == want.astype(F32)
        for part, kept in ((head, back_hi), (rest, back_lo)):
            value = jnp.where(hit, dot(part, spread), 0.0)
            for half in range(2):
                kept[chunk, pl.ds(half * rows, rows), :] = jnp.where(
                    half_of == half, value, 0.0
                ).astype(BF16)

    both = 2 * hidden_units

    def expert_chunk(slot, k):
        wait_chunk(arrived.at[slot], k, d_recv.at[slot], d_loc.at[slot])
        chunk = from_chunk(k)
        block = load_chunk(arrived.at[slot], chunk).astype(BF16)
        for half in range(2):
            where = (rows_of(chunk), pl.ds(half * both, both))
            total = dot(block, wgu[pieces[slot][half]])
            if slot == 0:
                acc[where] = total
            else:
                acc[where] += total

    def activate(chunk):
        first = acc[rows_of(chunk), pl.ds(0, both)]
        second = acc[rows_of(chunk), pl.ds(both, both)]
        total = first + pltpu.roll(second, chunk_rows - MOST_R, 0)
        inner = silu(total[:, :hidden_units]) * total[:, hidden_units:]
        _, half_of, _ = slot_parts((chunk_rows, hidden_units), 0)
        hid2[rows_of(chunk), pl.ds(0, hidden_units)] = jnp.where(
            half_of == 0, inner, 0.0
        ).astype(BF16)
        hid2[rows_of(chunk), pl.ds(hidden_units, hidden_units)] = jnp.where(
            half_of == 1, pltpu.roll(inner, MOST_R, 0), 0.0
        ).astype(BF16)

    partial = (outgoing.at[0], outgoing.at[1], for_left)

    def down(slot, owner, k):
        chunk = from_chunk(k)
        part = dot(hid2[rows_of(chunk), :], wed[owner])
        if slot is not None:
            partial[slot][pl.ds(chunk * per_chunk, per_chunk)] = part.reshape(
                per_chunk, 2 * MOST_R, wide
            ).astype(BF16)
        else:
            acc[rows_of(chunk), pl.ds(0, wide)] = part

    def e_copy(at, slot, k, landing, device):
        where = pl.ds(from_chunk(k) * per_chunk, per_chunk)
        return to(
            partial[slot].at[where],
            landing.at[where],
            e_send.at[at],
            e_recv.at[at],
            (dp, device),
        )

    relays, directs, passed = [], [], []
    for k in range(chunks):
        ahead, behind = ((1, right, e_left), (2, left, e_right))[:: 1 if k % 2 == 0 else -1]
        relays.append(e_copy(k, 0, k, e_relay, ahead[1]))
        directs.append(e_copy(4 + k, behind[0], k, behind[2], behind[1]))
        passed.append((ahead, e_copy(8 + k, ahead[0], k, ahead[2], ahead[1])))

    def pass_on(k):
        (slot, _, _), copy = passed[k]
        where = pl.ds(from_chunk(k) * per_chunk, per_chunk)
        relays[k].wait_recv()
        partial[slot][where] = (
            partial[slot][where].astype(F32) + e_relay[where].astype(F32)
        ).astype(BF16)
        copy.start()

    def finish(k):
        chunk = from_chunk(k)
        directs[k].wait_recv()
        passed[k][1].wait_recv()
        total = (
            acc[rows_of(chunk), pl.ds(0, wide)]
            + load_chunk(e_left, chunk)
            + load_chunk(e_right, chunk)
        )
        outgoing[2, pl.ds(chunk * per_chunk, per_chunk)] = total.reshape(
            per_chunk, 2 * MOST_R, wide
        ).astype(BF16)
        send_chunk(outgoing.at[2], came, chunk, c_send.at[0], c_recv.at[k], c_loc.at[0])

    first, second = range(chunks // 2), range(chunks // 2, chunks)
    for at in (0, 1):
        gathers[at].wait_recv()
        gathers[at + 2].start()
        gathers[at + 4].start()
    select(1)
    issue_next(*((1, k) for k in first))
    arrived_weights(wgu, 2)
    for k in range(chunks):
        expert_chunk(0, k)
    issue_next(*((1, k) for k in second))
    shared_step(1)
    for k in first:
        expert_chunk(1, k)
    for at in (2, 3):
        gathers[at].wait_recv()
    select(2)
    for copy in fetches:
        copy.wait_recv()

    @pl.loop(1, chunks)
    def _(step):
        piece = others.at[core, mine]
        device = spread_to(lax.rem(near + step, chunks), far)
        to(piece, piece, p_sem.at[0], p_sem.at[1], device).start()

    for at in (4, 5):
        gathers[at].wait_recv()
    select(3)
    issue_next((2, 0), (3, 0))
    shared_step(2)
    shared_step(3)

    shared_hidden = (
        silu(shared_acc[:, pl.ds(0, hidden_units)])
        * shared_acc[:, pl.ds(hidden_units, hidden_units)]
    ).astype(BF16)
    s_hidden[0] = shared_hidden
    hidden_sends = [
        to(
            s_hidden.at[0],
            s_hidden.at[place],
            s_send.at[3 + at],
            s_recv.at[3 + at],
            (dp, device),
        )
        for at, (device, place) in enumerate(((right, 3), (left, 1), (across, 2)))
    ]
    for copy in hidden_sends:
        copy.start()

    for k in second:
        expert_chunk(1, k)
    arrived_weights(wed, 4)

    def last_steps(k):
        expert_chunk(2, k)
        expert_chunk(3, k)
        activate(from_chunk(k))
        down(0, across, k)
        relays[k].start()
        slot, device = ((2, left), (1, right))[k % 2]
        down(slot, device, k)
        if k < chunks - 1:
            directs[k].start()
        (slot, device, _), _ = passed[k]
        down(slot, device, k)
        down(None, tp, k)

    for k in range(chunks):
        if k + 1 < chunks:
            issue_next((2, k + 1), (3, k + 1))
        last_steps(k)
        if k >= 1:
            pass_on(k - 1)
    wait_queue(len(queue))

    for k in range(chunks - 2):
        finish(k)
    wait_peers(others.at[core], p_sem.at[1], chunks - 1)

    @pl.loop(1, chunks)
    def _(step):
        line = others.at[core, pl.ds(far * chunks, chunks)]
        device = spread_to(near, lax.rem(far + step, chunks))
        to(line, line, p_sem.at[4], p_sem.at[5], device).start()

    passed[chunks - 2][1].wait_send()
    directs[chunks - 1].start()
    pass_on(chunks - 1)
    finish(chunks - 2)
    wait_peers(others.at[core], p_sem.at[5], chips - chunks)
    swap = to(
        others.at[core], others.at[core], p_sem.at[2], p_sem.at[3], (dp + 1 - 2 * core, tp)
    )
    swap.start()
    finish(chunks - 1)

    for copy in hidden_sends:
        copy.wait_recv()
    arrived_weights(wsd, 3)
    swap.wait_recv()
    for half in range(2):
        total = dot(s_hidden[0], wsd[half])
        for place in range(TP - 1):
            total += dot(
                s_hidden[place + 1], others[half, :, place].reshape(hidden_units, wide)
            )
        s_own[pl.ds(half * rows, rows)] = total

    for k in range(chunks):
        wait_chunk(came, k, c_recv, c_loc.at[0])
        chunk = chunk_at(k)
        block = load_chunk(came, chunk).astype(BF16)
        s_own[...] += dot(back_hi[chunk], block) + dot(back_lo[chunk], block)
    keep = lax.broadcasted_iota(jnp.int32, (rows, wide), 0) < length
    for half in range(2):
        out_ref[:, pl.ds(half * wide, wide)] = jnp.where(
            keep, s_own[pl.ds(half * rows, rows)], 0.0
        ).astype(out_ref.dtype)

    sends = gathers + fetches + hidden_sends + [swap]
    for copy in sends + relays + directs + [copy for k, (_, copy) in enumerate(passed) if k != chunks - 2]:
        copy.wait_send()
    wait_peers(others.at[core], p_sem.at[0], chunks - 1)
    wait_peers(others.at[core], p_sem.at[4], chips - chunks)
    wait_peers(outgoing.at[2], c_send.at[0], groups - 1)


def local(
    hidden_in,
    lengths,
    routes,
    route_weights,
    placement,
    shared_gate,
    shared_up,
    shared_down,
    expert_gate,
    expert_up,
    expert_down,
):
    groups = lax.axis_size("dp")
    rows, quarter = hidden_in.shape
    wide = quarter // 2
    pieces = 2 * TP
    units = shared_gate.shape[1]
    window = placement.shape[0]
    chunks = side_of(groups)
    packed = groups * 2 * MOST_R
    across_peers = (groups, 2 * MOST_R, wide)
    vmem = pl.BlockSpec(memory_space=pltpu.VMEM)
    smem = pl.BlockSpec(memory_space=pltpu.SMEM)
    hbm = pl.BlockSpec(memory_space=pl.ANY)
    dma = pltpu.SemaphoreType.DMA
    return pl.pallas_call(
        functools.partial(kernel, groups),
        out_shape=jax.ShapeDtypeStruct((rows, quarter), BF16),
        in_specs=[vmem] * 3 + [smem] + [hbm] * 7,
        out_specs=vmem,
        scratch_shapes=[
            pltpu.VMEM((pieces, wide, 2 * units), BF16),
            pltpu.VMEM((2, units, wide), BF16),
            pltpu.VMEM((pieces, wide, 2 * units), BF16),
            pltpu.VMEM((TP, 2 * units, wide), BF16),
            pltpu.VMEM((TP, 2 * rows, wide), BF16),
            pltpu.VMEM((packed, 2 * rows), BF16),
            pltpu.VMEM((chunks, 2 * rows, packed // chunks), BF16),
            pltpu.VMEM((chunks, 2 * rows, packed // chunks), BF16),
            pltpu.VMEM((TP,) + across_peers, BF16),
            pltpu.VMEM((TP,) + across_peers, BF16),
            pltpu.VMEM((packed, 4 * units), F32),
            pltpu.VMEM((rows, 2 * units), F32),
            pltpu.VMEM((packed, 2 * units), BF16),
            pltpu.VMEM((TP, rows, units), BF16),
            pltpu.VMEM((2 * rows, wide), F32),
            pltpu.VMEM((2, groups // 2, TP - 1, 2 * units // groups, wide), BF16),
            pltpu.VMEM(across_peers, BF16),
            pltpu.VMEM(across_peers, BF16),
            pltpu.VMEM(across_peers, BF16),
            pltpu.VMEM(across_peers, BF16),
            pltpu.VMEM(across_peers, BF16),
            dma((5,)),
            dma((6,)),
            dma((6,)),
            dma((TP, chunks)),
            dma((TP, chunks)),
            dma((TP,)),
            dma((6,)),
            dma((6,)),
            dma((6,)),
            dma((12,)),
            dma((12,)),
            dma((1,)),
            dma((chunks,)),
            dma((1,)),
        ],
        compiler_params=pltpu.CompilerParams(
            collective_id=0, has_side_effects=True, vmem_limit_bytes=62 << 20
        ),
        cost_estimate=pl.CostEstimate(
            flops=2 * 5 * rows * quarter * 4 * units * 3 // 2,
            bytes_accessed=6 * quarter * 4 * units * 2,
            transcendentals=0,
        ),
    )(
        routes.T,
        route_weights.T,
        placement.reshape(1, window),
        lengths,
        hidden_in,
        shared_gate.reshape(pieces, wide, units),
        shared_up.reshape(pieces, wide, units),
        shared_down,
        expert_gate.reshape(pieces, wide, units),
        expert_up.reshape(pieces, wide, units),
        expert_down[0],
    )


def solution(mesh):
    in_specs = (
        P("dp", "tp"),
        P("dp"),
        P("dp", None),
        P("dp", None),
        P(),
        P(None, "tp"),
        P(None, "tp"),
        P("tp", None),
        P("dp", None, "tp"),
        P("dp", None, "tp"),
        P("dp", "tp", None),
    )
    out_specs = P("dp", "tp")
    return jax.shard_map(local, mesh=mesh, in_specs=in_specs, out_specs=out_specs, check_vma=False)
```
